32 devices in a mesh: ctx: 8 (over y, x, core), tp: 4 (over z).
Axes of the slice: x: 2, y: 2, z: 4, core: 2. Of those that a mesh axis runs over, the one named last changes fastest.
Arguments:
- queries: bfloat16 [512, 8192], P('ctx', 'tp'), may hold values from -45 to 45
- key_rows: bfloat16 [512, 1024], P('ctx', 'tp'), may hold values from -6 to 6
- value_rows: bfloat16 [512, 1024], P('ctx', 'tp'), may hold values from -6 to 6
- out_weight: bfloat16 [8192, 5120], P('tp', 'ctx'), may hold values from -0.5 to 0.5
- stream: bfloat16 [512, 5120], P('tp', 'ctx'), may hold values from -18 to 18
- final_gain: bfloat16 [5120], replicated, may hold values from 0.5 to 1.5
- head_weight: bfloat16 [5120, 12288], P(None, ('ctx', 'tp')), may hold values from -1 to 1
- token_ids: int32 [512], replicated, may hold values from 0 to 12287
- policy_logprob: float32 [512], P('ctx'), may hold values from -20 to -10
- doc_lengths: int32 [64], replicated, may hold values from 1 to 8192, 131072 in all
- slab_start: int32 [1], replicated, may hold values from 0 to 130560
Outputs:
- ref_logprob: float32 [512], P('ctx')
- kl_penalty: float32 [512], P('ctx')
The draws below stay inside these ranges and needn't reach their ends.
All inputs are finite; a program needn't handle non-finite values.
Results may differ from the reference program's by a relative error of at most 0.017.
Values may be sent and summed in bfloat16 or wider, within the bound.
No kernel may reach another device: no remote copies, remote signals or barrier semaphores. Data moves between devices by JAX's collectives and lax.ppermute only.
A program may use at most 128 MiB of HBM per device.

```python
import math
import jax
import jax.numpy as jnp
import numpy as np
from jax import lax

D = 5120
HEADS = 64
KV_HEADS = 8
HD = 128
V_DEV = 384
Q_DEV = 64
ROW = 131072
DOCS = 64
MOST = 8192
SLAB = 512
VOCAB = 12288
N_CTX = 8
N_TP = 4


def attention_inputs(key):
    base = jax.random.fold_in(key, 5501)
    keys_draw = jax.random.normal(jax.random.fold_in(base, 1), (SLAB, KV_HEADS * HD), jnp.float32)
    query_draw = jax.random.normal(jax.random.fold_in(base, 2), (SLAB, HEADS * HD), jnp.float32)
    return (jnp.clip(query_draw, -45.0, 45.0), jnp.clip(keys_draw, -6.0, 6.0))


def draw_queries(key, part):
    return attention_inputs(key)[0].astype(jnp.bfloat16)


def draw_key_rows(key, part):
    return attention_inputs(key)[1].astype(jnp.bfloat16)


def draw_stream(key, part):
    base = jax.random.fold_in(key, 7707)
    rows_draw = jax.random.normal(jax.random.fold_in(base, 2), (SLAB, D), jnp.float32)
    return jnp.clip(rows_draw, -18.0, 18.0).astype(jnp.bfloat16)


def draw_head_weight(key, part):
    base = jax.random.fold_in(key, 7707)
    deviation = 3.0 / D ** 0.5
    table = jnp.clip(deviation * jax.random.normal(jax.random.fold_in(base, 5), (D, VOCAB), jnp.float32), -6.0 * deviation, 6.0 * deviation)
    return table.astype(jnp.bfloat16)


def draw_token_ids(key, part):
    base = jax.random.fold_in(key, 9109)
    positions = jnp.arange(SLAB, dtype=jnp.int32)
    owner = positions // (SLAB // N_CTX)
    device_count = N_CTX * N_TP
    shard = (owner * N_TP + positions // 2 % N_TP + device_count // 2) % device_count
    inside = jax.random.randint(jax.random.fold_in(base, 1), (SLAB,), 0, V_DEV, jnp.int32)
    anywhere = jax.random.randint(jax.random.fold_in(base, 2), (SLAB,), 0, VOCAB, jnp.int32)
    tokens = jnp.where(positions % 2 == 0, shard * V_DEV + inside, anywhere)
    tokens = jnp.where(positions == 1, VOCAB - 1, tokens)
    tokens = jnp.where(positions == 3, 0, tokens)
    return tokens.astype(jnp.int32)


def level_of(stream_key, extent, pieces, low, high):
    def one(position, blocks):
        steps = jax.random.uniform(jax.random.fold_in(jax.random.fold_in(stream_key, 6), position), (blocks,), jnp.float32, low / len(pieces), high / len(pieces))
        return jnp.repeat(jnp.exp(steps), extent[position] // blocks).reshape((-1,) + (1,) * (len(extent) - position - 1))

    factor_of = one(*pieces[0])
    for cut in pieces[1:]:
        factor_of = factor_of * one(*cut)
    return factor_of


def length_profile(count, total, most, slope):
    portions = [(1 << 20) // math.isqrt(rank ** slope) + 1 for rank in range(2, count + 1)]
    rest, holding = total - most - (count - 1), [1] * (count - 1)
    while rest > 0:
        candidates = [i for i in range(count - 1) if holding[i] < most]
        whole, remaining = sum([portions[i] for i in candidates]), rest
        for i in candidates:
            addition = min(most - holding[i], max(1, remaining * portions[i] // whole), rest)
            holding[i] = holding[i] + addition
            rest = rest - addition
    return np.array([most] + holding)


def ragged(key, count, total, bound, lean):
    if count == 2:
        one = jax.random.randint(key, (), max(1, total - bound), min(bound, total - 1) + 1)
        return jnp.stack([one, total - one])
    sizes = jnp.asarray(length_profile(count, total, bound, lean), jnp.int32)
    pairs = (count - 1) // 2
    giver, sink = sizes[1:1 + 2 * pairs:2], sizes[2:2 + 2 * pairs:2]
    room = jnp.minimum(giver - 1, bound - sink)
    shifted = jax.random.randint(jax.random.fold_in(key, 1), (pairs,), 0, 1 << 20) % (room + 1)
    sizes = sizes.at[1:1 + 2 * pairs:2].set(giver - shifted).at[2:2 + 2 * pairs:2].set(sink + shifted)
    return sizes[jax.random.permutation(jax.random.fold_in(key, 2), count)]


def normal_values(key, extent, scale, bound, shards=(), kind=jnp.bfloat16):
    drawn = scale * jax.random.normal(key, extent, jnp.float32)
    if shards:
        drawn = drawn * level_of(key, extent, shards, -0.22, 0.18)
    return jnp.clip(drawn, -bound, bound).astype(kind)


def setup_inputs(seed: int = 0) -> dict:
    seeds = jax.random.split(jax.random.key(seed), 12)
    return {
        "queries": draw_queries(jax.random.fold_in(seeds[11], 71), 0),
        "key_rows": draw_key_rows(jax.random.fold_in(seeds[11], 71), 0),
        "value_rows": normal_values(seeds[2], (SLAB, KV_HEADS * HD), 1.0, 6.0, ((0, 8), (1, 4))),
        "out_weight": normal_values(seeds[3], (HEADS * HD, D), HD ** -0.5, 0.5, ((0, 4), (1, 8))),
        "stream": draw_stream(jax.random.fold_in(seeds[11], 71), 0),
        "final_gain": jnp.clip(1.0 + 0.1 * jax.random.normal(seeds[5], (D,), jnp.float32), 0.5, 1.5).astype(jnp.bfloat16),
        "head_weight": draw_head_weight(jax.random.fold_in(seeds[11], 71), 0),
        "token_ids": draw_token_ids(jax.random.fold_in(seeds[11], 71), 0),
        "policy_logprob": jnp.clip(-20.0 + 10.0 * jax.random.uniform(seeds[8], (SLAB,), jnp.float32) ** level_of(seeds[8], (SLAB,), ((0, 8),), -0.2, 0.2), -20.0, -10.0),
        "doc_lengths": ragged(seeds[9], DOCS, ROW, MOST, 2).astype(jnp.int32),
        "slab_start": jax.random.randint(seeds[10], (1,), 0, ROW - Q_DEV * N_CTX + 1).astype(jnp.int32),
    }


EPSILON = 1e-06
CEILING = 10.0
NEGATIVE = -1e+30

def reference(queries, key_rows, value_rows, out_weight, stream, final_gain, head_weight, token_ids, policy_logprob, doc_lengths, slab_start):
    doc_ends = jnp.cumsum(doc_lengths)
    places = slab_start[0] + jnp.arange(SLAB, dtype=jnp.int32)
    docs = lax.optimization_barrier(jnp.sum((doc_ends[None, :] <= places[:, None]).astype(jnp.int32), axis=1))
    positions = jnp.arange(SLAB, dtype=jnp.int32)
    allowed = (positions[None, :] <= positions[:, None]) & (docs[None, :] == docs[:, None])
    group_size = HEADS // KV_HEADS

    def one_head(head):
        query = lax.dynamic_slice_in_dim(queries, (head * HD).astype(jnp.int32), HD, 1)
        shared = head // group_size * HD
        key_block = lax.dynamic_slice_in_dim(key_rows, shared.astype(jnp.int32), HD, 1)
        value_block = lax.dynamic_slice_in_dim(value_rows, shared.astype(jnp.int32), HD, 1)
        scores = jnp.dot(query, key_block.T, preferred_element_type=jnp.float32) * HD ** (-0.5)
        scores = jnp.where(allowed, scores, NEGATIVE)
        highest = lax.optimization_barrier(jnp.max(scores, axis=1, keepdims=True))
        weights = jnp.where(allowed, jnp.exp(scores - highest), 0.0)
        denominator = lax.optimization_barrier(jnp.sum(weights, axis=1, keepdims=True))
        mixed = jnp.dot(weights.astype(jnp.bfloat16), value_block, preferred_element_type=jnp.float32)
        return mixed / denominator
    heads_all = lax.map(one_head, jnp.arange(HEADS, dtype=jnp.int32))
    attended = heads_all.transpose(1, 0, 2).reshape(SLAB, HEADS * HD).astype(jnp.bfloat16)
    projected = jnp.dot(attended, out_weight, preferred_element_type=jnp.float32)
    updated = (stream.astype(jnp.float32) + projected).astype(jnp.bfloat16)
    wide = updated.astype(jnp.float32)
    inverse = lax.rsqrt(lax.optimization_barrier(jnp.mean(wide * wide, axis=1)) + EPSILON)
    normed = (wide * inverse[:, None] * final_gain.astype(jnp.float32)).astype(jnp.bfloat16)
    block_width = V_DEV * N_TP

    def vocab_step(running, index):
        highest, denominator = running
        weight_block = lax.dynamic_slice_in_dim(head_weight, (index * block_width).astype(jnp.int32), block_width, 1)
        logits = jnp.dot(normed, weight_block, preferred_element_type=jnp.float32)
        joined = jnp.maximum(highest, lax.optimization_barrier(jnp.max(logits, axis=1)))
        denominator = denominator * jnp.exp(highest - joined) + lax.optimization_barrier(jnp.sum(jnp.exp(logits - joined[:, None]), axis=1))
        return ((joined, denominator), None)
    starting = (jnp.full((SLAB,), NEGATIVE, jnp.float32), jnp.zeros((SLAB,), jnp.float32))
    (highest, denominator), unused = lax.scan(vocab_step, starting, jnp.arange(N_CTX, dtype=jnp.int32))
    picked = jnp.take(head_weight, token_ids, axis=1)
    target = lax.optimization_barrier(jnp.sum(normed.astype(jnp.float32) * picked.T.astype(jnp.float32), axis=1))
    normalizer = highest + jnp.log(denominator)
    ref_logprob = target - normalizer
    ratio_log = ref_logprob - policy_logprob
    kl_penalty = jnp.minimum(jnp.exp(ratio_log) - ratio_log - 1.0, CEILING)
    return (ref_logprob, kl_penalty)
```

```python
import jax
import jax.numpy as jnp
from jax import lax
from jax.experimental import pallas as pl
from jax.experimental.pallas import tpu as pltpu
from jax.sharding import PartitionSpec as P

HD = 128
EPSILON = 1e-06
CEILING = 10.0
NEGATIVE = -1e30
F32 = jnp.float32
BF16 = jnp.bfloat16
VMEM = pl.BlockSpec(memory_space=pltpu.VMEM)
SMEM = pl.BlockSpec(memory_space=pltpu.SMEM)
ANY = pl.BlockSpec(memory_space=pl.ANY)


def swap(x, axis, k):
    size = lax.axis_size(axis)
    return lax.ppermute(x, axis, [(i, i ^ k) for i in range(size)])


def gather_plane(pair, chips):
    first, second = pair
    if chips != 4:
        return [pair] + [(swap(first, "ctx", 2 * j), swap(second, "ctx", 2 * j)) for j in range(1, chips)]
    x0, y0 = swap(first, "ctx", 2), swap(first, "ctx", 4)
    x1, y1 = swap(second, "ctx", 2), swap(second, "ctx", 4)
    return [pair, (x0, x1), (y0, y1), (swap(y0, "ctx", 2), swap(x1, "ctx", 4))]


def attend_kernel(chips, tp_count, own_rows, blocks, place_ref, lens_ref, *refs):
    queries = refs[: 2 * chips]
    pairs = refs[2 * chips : 3 * chips]
    sibling_ref, w_own_ref, w_sib_ref = refs[3 * chips : 3 * chips + 3]
    outs = refs[3 * chips + 3 : 3 * chips + 3 + tp_count]
    keys, values, mixed, w_own, w_sib, product, sems = refs[3 * chips + 3 + tp_count :]
    copies = [
        pltpu.make_async_copy(w_own_ref, w_own, sems.at[0]),
        pltpu.make_async_copy(w_sib_ref, w_sib, sems.at[1]),
    ]
    for copy in copies:
        copy.start()
    ctx, tp, slab_start = place_ref[0], place_ref[1], place_ref[2]
    kv_width = keys.shape[1]
    kv_heads = kv_width // HD
    group = queries[0].shape[1] * 2 // kv_width
    length = keys.shape[0]
    for j in range(chips):
        own_at = pl.ds(pl.multiple_of((ctx ^ (2 * j)) * own_rows, own_rows), own_rows)
        sib_at = pl.ds(pl.multiple_of((ctx ^ (2 * j + 1)) * own_rows, own_rows), own_rows)
        keys[own_at, :] = pairs[j][:, :kv_width]
        values[own_at, :] = pairs[j][:, kv_width:]
        rows = slice(j * own_rows, (j + 1) * own_rows)
        keys[sib_at, :] = sibling_ref[rows, :kv_width]
        values[sib_at, :] = sibling_ref[rows, kv_width:]

    count = lens_ref.shape[0]
    before = lax.broadcasted_iota(jnp.int32, (count, count), 0) <= lax.broadcasted_iota(jnp.int32, (count, count), 1)
    ends = jnp.sum(jnp.where(before, lens_ref[...], 0), axis=0, keepdims=True)
    columns = lax.broadcasted_iota(jnp.int32, (own_rows, length), 1)
    for j in range(chips):
        spot = (ctx ^ (2 * j)) * own_rows + lax.broadcasted_iota(jnp.int32, (own_rows, 1), 0)
        opened = jnp.max(jnp.where(ends <= spot + slab_start, ends, 0), axis=1, keepdims=True) - slab_start
        allowed = ((columns <= spot) & (columns >= opened))[None]
        for h in range(kv_heads):
            heads = []
            for g in range(group):
                half, inner = divmod((h * group + g) * HD, queries[0].shape[1])
                heads.append(queries[2 * j + half][:, inner : inner + HD])
            stack = jnp.concatenate(heads, axis=0)
            scores = lax.dot_general(
                stack, keys[:, h * HD : (h + 1) * HD], (((1,), (1,)), ((), ())), preferred_element_type=F32
            ).reshape(group, own_rows, length)
            scores = jnp.where(allowed, scores, NEGATIVE)
            highest = jnp.max(scores, axis=2, keepdims=True)
            weights = jnp.exp((scores - highest) * HD ** (-0.5))
            denominator = jnp.sum(weights, axis=2, keepdims=True).reshape(group * own_rows, 1)
            mix = jnp.dot(
                weights.reshape(group * own_rows, length).astype(BF16),
                values[:, h * HD : (h + 1) * HD],
                preferred_element_type=F32,
            )
            mix = (mix / denominator).astype(BF16)
            for g in range(group):
                at = (h * group + g) * HD
                mixed[j * own_rows : (j + 1) * own_rows, at : at + HD] = mix[g * own_rows : (g + 1) * own_rows]
    for copy in copies:
        copy.wait()
    width = w_own.shape[1]
    product[:, :width] = jnp.dot(mixed[...], w_own[...], preferred_element_type=F32)
    product[:, width:] = jnp.dot(mixed[...], w_sib[...], preferred_element_type=F32)
    for k in range(tp_count):
        for b in range(blocks // 2):
            wanted = (tp ^ k) * blocks + 2 * b + lax.rem(ctx, 2)
            at = pl.multiple_of(lax.shift_right_logical(wanted ^ ctx, 1) * own_rows, own_rows)
            outs[k][b * own_rows : (b + 1) * own_rows, :] = product[pl.ds(at, own_rows), :].astype(outs[k].dtype)


def attend(place, lens, queries, pairs, sibling, w_own, w_sib, tp_count, blocks):
    chips, own_rows = len(pairs), pairs[0].shape[0]
    kv_width = pairs[0].shape[1] // 2
    length, plane_rows = 2 * chips * own_rows, chips * own_rows
    depth, width = w_own.shape
    out_rows = blocks // 2 * own_rows
    need = 4 * depth * width + 4 * plane_rows * (2 * depth + 2 * 2 * width) + 24 * 8 * own_rows * length
    return pl.pallas_call(
        lambda *refs: attend_kernel(chips, tp_count, own_rows, blocks, *refs),
        out_shape=[jax.ShapeDtypeStruct((out_rows, 2 * width), F32 if k == 0 else BF16) for k in range(tp_count)],
        in_specs=[SMEM] + [VMEM] * (2 + 3 * chips) + [ANY, ANY],
        out_specs=[VMEM] * tp_count,
        scratch_shapes=[
            pltpu.VMEM((length, kv_width), BF16),
            pltpu.VMEM((length, kv_width), BF16),
            pltpu.VMEM((plane_rows, depth), BF16),
            pltpu.VMEM((depth, width), BF16),
            pltpu.VMEM((depth, width), BF16),
            pltpu.VMEM((plane_rows, 2 * width), F32),
            pltpu.SemaphoreType.DMA((2,)),
        ],
        compiler_params=pltpu.CompilerParams(vmem_limit_bytes=need + (12 << 20)),
        name="attend",
    )(place, lens, *[q for two in queries for q in two], *pairs, sibling, w_own, w_sib)


def score_kernel(chips, tp_count, own_rows, blocks, place_ref, tokens_ref, gain_ref, *refs):
    halves = refs[: 2 * chips]
    h_own_ref, h_sib_ref, out_ref, head, normed, sems = refs[2 * chips :]
    ctx, tp = place_ref[0], place_ref[1]
    ranks = 2 * chips
    part, vocab = h_own_ref.shape[0] // ranks, h_own_ref.shape[1]
    copies = []
    for k in range(ranks):
        source = pl.ds(pl.multiple_of((ctx ^ k) * part, part), part)
        target = slice(k * part, (k + 1) * part)
        copies.append(pltpu.make_async_copy(h_own_ref.at[source], head.at[target, :vocab], sems.at[0, k]))
        copies.append(pltpu.make_async_copy(h_sib_ref.at[source], head.at[target, vocab:], sems.at[1, k]))
    for copy in copies:
        copy.start()
    half_rows = halves[0].shape[0]
    squares = [jnp.zeros((half_rows, 1), F32), jnp.zeros((half_rows, 1), F32)]
    for j in range(chips):
        gain = jnp.concatenate([gain_ref[pl.ds(ctx ^ (2 * j), 1), :], gain_ref[pl.ds(ctx ^ (2 * j + 1), 1), :]], axis=1)
        for s in range(2):
            wide = halves[2 * j + s][...].astype(F32)
            squares[s] += jnp.sum(wide * wide, axis=1, keepdims=True)
            normed[s * half_rows : (s + 1) * half_rows, 2 * j * part : 2 * (j + 1) * part] = (wide * gain).astype(BF16)
    square = jnp.concatenate(squares, axis=0)
    inverse = lax.rsqrt(square * (1.0 / (ranks * part)) + EPSILON)
    for copy in copies:
        copy.wait()
    logits = jnp.dot(normed[...], head[...], preferred_element_type=F32) * inverse
    rows = logits.shape[0]
    column = lax.broadcasted_iota(jnp.int32, (1, 2 * vocab), 1)
    offset = jnp.where(column < vocab, (ctx * tp_count + tp) * vocab, ((ctx ^ 1) * tp_count + tp) * vocab - vocab)
    owners = [
        (tp ^ k) * blocks + 2 * b + lax.rem(ctx, 2) for k in range(tp_count) for b in range(blocks // 2)
    ]
    tokens = jnp.concatenate(
        [tokens_ref[pl.ds(pl.multiple_of(owner * own_rows, own_rows), own_rows), :] for owner in owners], axis=0
    )
    highest = jnp.max(logits, axis=1, keepdims=True)
    total = jnp.sum(jnp.exp(logits - highest), axis=1, keepdims=True)
    target = jnp.sum(jnp.where(column + offset == tokens, logits, 0.0), axis=1, keepdims=True)
    lane = lax.broadcasted_iota(jnp.int32, (rows, 128), 1)
    packed = jnp.where(lane == 0, highest, jnp.where(lane == 1, total, jnp.where(lane == 2, target, 0.0)))
    turned = packed.T[:8]
    out_ref[...] = jnp.zeros(out_ref.shape, F32)
    for i, owner in enumerate(owners):
        tile = turned[:, i * own_rows : (i + 1) * own_rows]
        for k in range(tp_count):
            out_ref[pl.ds(owner * tp_count + k, 1), :, :own_rows] = tile[None]


def score(place, tokens, gain, halves, h_own, h_sib, tp_count, own_rows, blocks):
    chips = len(halves)
    half_rows, both = halves[0][0].shape
    depth, vocab = h_own.shape
    need = 4 * depth * vocab + 2 * half_rows * depth * 6 + 2 * half_rows * vocab * 2 * 4 * 8
    return pl.pallas_call(
        lambda *refs: score_kernel(chips, tp_count, own_rows, blocks, *refs),
        out_shape=jax.ShapeDtypeStruct((2 * chips * tp_count, 8, 128), F32),
        in_specs=[SMEM] + [VMEM] * (2 + 2 * chips) + [ANY, ANY],
        out_specs=VMEM,
        scratch_shapes=[
            pltpu.VMEM((depth, 2 * vocab), BF16),
            pltpu.VMEM((2 * half_rows, depth), BF16),
            pltpu.SemaphoreType.DMA((2, 2 * chips)),
        ],
        compiler_params=pltpu.CompilerParams(vmem_limit_bytes=need + (12 << 20)),
        name="score",
    )(place, tokens, gain, *[h for two in halves for h in two], h_own, h_sib)


def merge_kernel(chips, tp_count, place_ref, policy_ref, stats_ref, logprob_ref, penalty_ref):
    parity = lax.rem(place_ref[0], 2)
    own_rows = policy_ref.shape[1]
    tiles = [
        stats_ref[(2 * j + parity) * tp_count + k] for j in range(chips) for k in range(tp_count)
    ]
    highest = tiles[0][0:1]
    for tile in tiles[1:]:
        highest = jnp.maximum(highest, tile[0:1])
    total = jnp.zeros_like(highest)
    target = jnp.zeros_like(highest)
    for tile in tiles:
        total += tile[1:2] * jnp.exp(tile[0:1] - highest)
        target += tile[2:3]
    logprob = (target - (highest + jnp.log(total)))[:, :own_rows]
    ratio = logprob - policy_ref[...]
    logprob_ref[...] = logprob
    penalty_ref[...] = jnp.minimum(jnp.exp(ratio) - ratio - 1.0, CEILING)


def merge(place, policy, stats, chips, tp_count):
    shape = jax.ShapeDtypeStruct(policy.shape, F32)
    return pl.pallas_call(
        lambda *refs: merge_kernel(chips, tp_count, *refs),
        out_shape=[shape, shape],
        in_specs=[SMEM, VMEM, VMEM],
        out_specs=[VMEM, VMEM],
        name="merge",
    )(place, policy, stats)


def local(
    queries,
    key_rows,
    value_rows,
    out_weight,
    stream,
    final_gain,
    head_weight,
    token_ids,
    policy_logprob,
    doc_lengths,
    slab_start,
):
    ctx_count, tp_count = lax.axis_size("ctx"), lax.axis_size("tp")
    ctx, tp = lax.axis_index("ctx"), lax.axis_index("tp")
    core = lax.rem(ctx, 2)
    chips = ctx_count // 2
    own_rows = queries.shape[0]
    blocks = ctx_count // tp_count
    place = jnp.stack([ctx, tp, slab_start[0]]).astype(jnp.int32)

    pair = jnp.concatenate([key_rows, value_rows], axis=1)
    pairs = [pair] + [swap(pair, "ctx", 2 * j) for j in range(1, chips)]
    half = queries.shape[1] // 2
    query_sets = gather_plane((queries[:, :half], queries[:, half:]), chips)
    sibling = swap(jnp.concatenate(pairs, axis=0), "ctx", 1)
    out_sibling = swap(out_weight, "ctx", 1)
    head_sibling = swap(head_weight, "ctx", 1)
    cut = stream.reshape(blocks // 2, 2, own_rows, stream.shape[1])
    kept = lax.dynamic_index_in_dim(cut, core, 1, keepdims=False)
    given = lax.dynamic_index_in_dim(cut, 1 - core, 1, keepdims=False)
    stream_rows = jnp.concatenate([kept, swap(given, "ctx", 1)], axis=2).reshape(blocks // 2 * own_rows, -1)

    sums = attend(
        place, doc_lengths[:, None], query_sets, pairs, sibling, out_weight, out_sibling, tp_count, blocks
    )
    total = stream_rows.astype(F32) + sums[0]
    for k in range(1, tp_count):
        total = total + swap(sums[k], "tp", k).astype(F32)
    updated = total.astype(BF16)
    near = [updated] + [swap(updated, "tp", k) for k in range(1, tp_count)]
    mid = tp_count // 2
    halves = gather_plane((jnp.concatenate(near[:mid], axis=0), jnp.concatenate(near[mid:], axis=0)), chips)
    gain = final_gain.astype(F32).reshape(ctx_count, -1)
    stats = score(
        place, token_ids[:, None], gain, halves, head_weight, head_sibling, tp_count, own_rows, blocks
    )
    stats = lax.all_to_all(stats, ("ctx", "tp"), 0, 0, tiled=True)
    logprob, penalty = merge(place, policy_logprob[None], stats, chips, tp_count)
    return (logprob[0], penalty[0])


def solution(mesh):
    placed = (
        P("ctx", "tp"),
        P("ctx", "tp"),
        P("ctx", "tp"),
        P("tp", "ctx"),
        P("tp", "ctx"),
        P(),
        P(None, ("ctx", "tp")),
        P(),
        P("ctx"),
        P(),
        P(),
    )
    return jax.shard_map(
        local, mesh=mesh, in_specs=placed, out_specs=(P("ctx"), P("ctx")), check_vma=False
    )
```

```python
import jax
import jax.numpy as jnp
from jax import lax
from jax.experimental import pallas as pl
from jax.experimental.pallas import tpu as pltpu
from jax.sharding import PartitionSpec as P

HD = 128
EPSILON = 1e-06
CEILING = 10.0
NEGATIVE = -1e30
F32 = jnp.float32
BF16 = jnp.bfloat16
VMEM = pl.BlockSpec(memory_space=pltpu.VMEM)
SMEM = pl.BlockSpec(memory_space=pltpu.SMEM)
HBM = pl.BlockSpec(memory_space=pltpu.HBM)
ANY = pl.BlockSpec(memory_space=pl.ANY)


def swap(x, axis, k):
    size = lax.axis_size(axis)
    return lax.ppermute(x, axis, [(i, i ^ k) for i in range(size)])


def sides(piece, chips):
    if chips != 4:
        return [piece] + [swap(piece, "ctx", 2 * j) for j in range(1, chips)]
    return [piece, swap(piece, "ctx", 2), swap(piece, "ctx", 4)]


def corners(found, turn):
    if len(found) != 3:
        return found
    return [*found, swap(found[2 - turn], "ctx", 2 + 2 * turn)]


def attend_kernel(counts, tp_count, own_rows, kv_width, ks, blocks, place_ref, after_ref, lens_ref, weight_ref, *refs):
    chips, total = len(counts), sum(counts)
    outs = refs[total : total + len(ks)]
    queries, keys, values, mixed = refs[total + len(ks) :]
    ctx, tp, slab_start = place_ref[0], place_ref[1], place_ref[2]
    kv_heads = kv_width // HD
    depth = queries.shape[1]
    group = depth // kv_width
    length = keys.shape[0]
    owners = [(tp ^ k) * blocks + 2 * b + lax.rem(ctx, 2) for k in ks for b in range(blocks // 2)]
    for j in range(chips):
        parts = refs[sum(counts[:j]) : sum(counts[: j + 1])]
        if parts[0].shape[1] == depth:
            spans = [(parts[0], 0, 0, depth)]
            own, sib, start = parts[1], parts[1], 2 * kv_width
            at = 0
        else:
            half = depth // 2
            spans = [(parts[0], 0, 0, half), (parts[1], 0, half, half)]
            own, sib, start = parts[0], parts[1], half
            at = half
        own_at = pl.ds(pl.multiple_of((ctx ^ (2 * j)) * own_rows, own_rows), own_rows)
        sib_at = pl.ds(pl.multiple_of((ctx ^ (2 * j + 1)) * own_rows, own_rows), own_rows)
        for rows, part, first in ((own_at, own, at), (sib_at, sib, start)):
            keys[rows, :] = part[:, first : first + kv_width]
            values[rows, :] = part[:, first + kv_width : first + 2 * kv_width]
        for i, owner in enumerate(owners):

            @pl.when(owner == (ctx ^ (2 * j)))
            def _(spans=spans, i=i):
                for part, first, target, width in spans:
                    queries[i * own_rows : (i + 1) * own_rows, target : target + width] = part[:, first : first + width]

    count = lens_ref.shape[1]
    first = lax.broadcasted_iota(jnp.int32, (count, count), 0)
    second = lax.broadcasted_iota(jnp.int32, (count, count), 1)
    column = jnp.sum(jnp.where(first == second, lens_ref[...], 0), axis=1, keepdims=True)
    ends = jnp.sum(jnp.where(first <= second, column, 0), axis=0, keepdims=True)
    columns = lax.broadcasted_iota(jnp.int32, (own_rows, length), 1)
    for i, owner in enumerate(owners):
        spot = owner * own_rows + lax.broadcasted_iota(jnp.int32, (own_rows, 1), 0)
        opened = jnp.max(jnp.where(ends <= spot + slab_start, ends, 0), axis=1, keepdims=True) - slab_start
        allowed = ((columns <= spot) & (columns >= opened))[None]
        at = slice(i * own_rows, (i + 1) * own_rows)
        for h in range(kv_heads):
            heads = [(h * group + g) * HD for g in range(group)]
            stack = jnp.concatenate([queries[at, head : head + HD] for head in heads], axis=0)
            scores = lax.dot_general(
                stack, keys[:, h * HD : (h + 1) * HD], (((1,), (1,)), ((), ())), preferred_element_type=F32
            ).reshape(group, own_rows, length)
            scores = jnp.where(allowed, scores, NEGATIVE)
            highest = jnp.max(scores, axis=2, keepdims=True)
            weights = jnp.exp((scores - highest) * HD ** (-0.5))
            denominator = jnp.sum(weights, axis=2, keepdims=True).reshape(group * own_rows, 1)
            mix = jnp.dot(
                weights.reshape(group * own_rows, length).astype(BF16),
                values[:, h * HD : (h + 1) * HD],
                preferred_element_type=F32,
            )
            mix = (mix / denominator).astype(BF16)
            for g, head in enumerate(heads):
                mixed[i * own_rows : (i + 1) * own_rows, head : head + HD] = mix[g * own_rows : (g + 1) * own_rows]
    product = jnp.dot(mixed[...], weight_ref[...], preferred_element_type=F32)
    span = blocks // 2 * own_rows
    for i, out in enumerate(outs):
        out[...] = product[i * span : (i + 1) * span].astype(out.dtype)


def attend(place, after, lens, sets, kv_width, weight, ks, tp_count, blocks):
    chips, own_rows = len(sets), sets[0][0].shape[0]
    length = 2 * chips * own_rows
    depth, width = weight.shape
    span = blocks // 2 * own_rows
    rows = len(ks) * span
    need = 2 * depth * width + chips * own_rows * depth * 2 + rows * (depth * 4 + width * 16) + 24 * 8 * own_rows * length
    return pl.pallas_call(
        lambda *refs: attend_kernel([len(one) for one in sets], tp_count, own_rows, kv_width, ks, blocks, *refs),
        out_shape=[jax.ShapeDtypeStruct((span, width), F32 if k == 0 else BF16) for k in ks],
        in_specs=[SMEM, ANY] + [VMEM] * (2 + sum(len(one) for one in sets)),
        out_specs=[VMEM] * len(ks),
        scratch_shapes=[
            pltpu.VMEM((rows, depth), BF16),
            pltpu.VMEM((length, kv_width), BF16),
            pltpu.VMEM((length, kv_width), BF16),
            pltpu.VMEM((rows, depth), BF16),
        ],
        compiler_params=pltpu.CompilerParams(vmem_limit_bytes=need + (8 << 20)),
        name="attend",
    )(place, after, lens, weight, *[part for one in sets for part in one])


def update_kernel(blocks, own_rows, place_ref, after_ref, stream_ref, stream_sib_ref, *refs):
    sums, out_ref = refs[:-1], refs[-1]
    core = lax.rem(place_ref[0], 2)
    width = stream_ref.shape[1]
    for b in range(blocks // 2):
        source = pl.ds(pl.multiple_of((2 * b + core) * own_rows, own_rows), own_rows)
        target = slice(b * own_rows, (b + 1) * own_rows)
        for side, part in enumerate((stream_ref, stream_sib_ref)):
            columns = slice(side * width, (side + 1) * width)
            total = part[source, :].astype(F32)
            for one in sums:
                total += one[target, columns].astype(F32)
            out_ref[target, columns] = total.astype(BF16)


def update(place, after, stream, stream_sib, sums, blocks, own_rows):
    return pl.pallas_call(
        lambda *refs: update_kernel(blocks, own_rows, *refs),
        out_shape=jax.ShapeDtypeStruct(sums[0].shape, BF16),
        in_specs=[SMEM, ANY] + [VMEM] * (2 + len(sums)),
        out_specs=VMEM,
        compiler_params=pltpu.CompilerParams(vmem_limit_bytes=6 << 20),
        name="update",
    )(place, after, stream, stream_sib, *sums)


def stage_kernel(place_ref, own_ref, sib_ref, both_ref, mark_ref, sems):
    ranks = sems.shape[1]
    part, width = own_ref.shape[0] // ranks, own_ref.shape[1]
    mark_ref[...] = jnp.zeros(mark_ref.shape, F32)
    if width % 128:
        for k in range(ranks):
            source = pl.ds(pl.multiple_of((place_ref[0] ^ k) * part, part), part) if ranks > 1 else slice(0, part)
            both_ref[k * part : (k + 1) * part, :width] = own_ref[source, :]
            both_ref[k * part : (k + 1) * part, width:] = sib_ref[source, :]
        return
    copies = []
    for k in range(ranks):
        source = pl.ds(pl.multiple_of((place_ref[0] ^ k) * part, part), part) if ranks > 1 else slice(0, part)
        target = slice(k * part, (k + 1) * part)
        copies.append(pltpu.make_async_copy(own_ref.at[source], both_ref.at[target, :width], sems.at[0, k]))
        copies.append(pltpu.make_async_copy(sib_ref.at[source], both_ref.at[target, width:], sems.at[1, k]))
    for copy in copies:
        copy.start()
    for copy in copies:
        copy.wait()


def stage(place, own, sib, ranks):
    depth, width = own.shape
    return pl.pallas_call(
        stage_kernel,
        out_shape=[jax.ShapeDtypeStruct((depth, 2 * width), BF16), jax.ShapeDtypeStruct((8, 128), F32)],
        in_specs=[SMEM] + [VMEM if width % 128 else HBM] * 2,
        out_specs=[VMEM, VMEM],
        scratch_shapes=[pltpu.SemaphoreType.DMA((2, ranks))],
        compiler_params=pltpu.CompilerParams(vmem_limit_bytes=(8 if width % 128 else 4) * depth * width + (4 << 20)),
        name="stage",
    )(place, own, sib)


def score_kernel(chips, tp_count, own_rows, blocks, first, place_ref, tokens_ref, gain_ref, head_ref, *refs):
    pieces, out_ref, normed = refs[:-2], refs[-2], refs[-1]
    spans = len(pieces) // chips
    ctx, tp = place_ref[0], place_ref[1]
    ranks = 2 * chips
    part, vocab = head_ref.shape[0] // ranks, head_ref.shape[1] // 2
    span_rows = pieces[0].shape[0]
    squares = [jnp.zeros((span_rows, 1), F32)] * spans
    for j in range(chips):
        gain = jnp.concatenate([gain_ref[pl.ds(ctx ^ (2 * j), 1), :], gain_ref[pl.ds(ctx ^ (2 * j + 1), 1), :]], axis=1)
        for s in range(spans):
            wide = pieces[s * chips + j][...].astype(F32)
            squares[s] += jnp.sum(wide * wide, axis=1, keepdims=True)
            normed[s * span_rows : (s + 1) * span_rows, 2 * j * part : 2 * (j + 1) * part] = (wide * gain).astype(BF16)
    square = jnp.concatenate(squares, axis=0)
    inverse = lax.rsqrt(square * (1.0 / (ranks * part)) + EPSILON)
    logits = jnp.dot(normed[...], head_ref[...], preferred_element_type=F32) * inverse
    rows = logits.shape[0]
    column = lax.broadcasted_iota(jnp.int32, (1, 2 * vocab), 1)
    offset = jnp.where(column < vocab, (ctx * tp_count + tp) * vocab, ((ctx ^ 1) * tp_count + tp) * vocab - vocab)
    owners = [
        (tp ^ k) * blocks + 2 * b + lax.rem(ctx, 2) for k in range(first, first + spans) for b in range(blocks // 2)
    ]
    length = tokens_ref.shape[1]
    line = lax.broadcasted_iota(jnp.int32, (own_rows, length), 1) - lax.broadcasted_iota(jnp.int32, (own_rows, length), 0)
    tokens = jnp.concatenate(
        [
            jnp.sum(jnp.where(line == owner * own_rows, tokens_ref[...], 0), axis=1, keepdims=True)
            for owner in owners
        ],
        axis=0,
    )
    highest = jnp.max(logits, axis=1, keepdims=True)
    total = jnp.sum(jnp.exp(logits - highest), axis=1, keepdims=True)
    target = jnp.sum(jnp.where(column + offset == tokens, logits, 0.0), axis=1, keepdims=True)
    lane = lax.broadcasted_iota(jnp.int32, (rows, 128), 1)
    packed = jnp.where(lane == 0, highest, jnp.where(lane == 1, total, jnp.where(lane == 2, target, 0.0)))
    turned = packed.T[:8]
    out_ref[...] = jnp.zeros(out_ref.shape, F32)
    for i, owner in enumerate(owners):
        tile = turned[:, i * own_rows : (i + 1) * own_rows]
        for k in range(tp_count):
            out_ref[pl.ds(owner * tp_count + k, 1), :, :own_rows] = tile[None]


def score(place, tokens, gain, head, spans, first, tp_count, own_rows, blocks):
    chips = len(spans[0])
    rows = len(spans) * spans[0][0].shape[0]
    depth, vocab = head.shape
    need = 2 * depth * vocab + rows * depth * 6 + rows * vocab * 4 * 8
    return pl.pallas_call(
        lambda *refs: score_kernel(chips, tp_count, own_rows, blocks, first, *refs),
        out_shape=jax.ShapeDtypeStruct((2 * chips * tp_count, 8, 128), F32),
        in_specs=[SMEM] + [VMEM] * (3 + len(spans) * chips),
        out_specs=VMEM,
        scratch_shapes=[pltpu.VMEM((rows, depth), BF16)],
        compiler_params=pltpu.CompilerParams(vmem_limit_bytes=need + (12 << 20)),
        name="score",
    )(place, tokens, gain, head, *[piece for span in spans for piece in span])


def merge_kernel(chips, tp_count, place_ref, policy_ref, stats_ref, logprob_ref, penalty_ref):
    parity = lax.rem(place_ref[0], 2)
    own_rows = policy_ref.shape[1]
    tiles = [
        stats_ref[(2 * j + parity) * tp_count + k] for j in range(chips) for k in range(tp_count)
    ]
    highest = tiles[0][0:1]
    for tile in tiles[1:]:
        highest = jnp.maximum(highest, tile[0:1])
    total = jnp.zeros_like(highest)
    target = jnp.zeros_like(highest)
    for tile in tiles:
        total += tile[1:2] * jnp.exp(tile[0:1] - highest)
        target += tile[2:3]
    logprob = (target - (highest + jnp.log(total)))[:, :own_rows]
    ratio = logprob - policy_ref[...]
    logprob_ref[...] = logprob
    penalty_ref[...] = jnp.minimum(jnp.exp(ratio) - ratio - 1.0, CEILING)


def merge(place, policy, stats, chips, tp_count):
    shape = jax.ShapeDtypeStruct(policy.shape, F32)
    return pl.pallas_call(
        lambda *refs: merge_kernel(chips, tp_count, *refs),
        out_shape=[shape, shape],
        in_specs=[SMEM, VMEM, VMEM],
        out_specs=[VMEM, VMEM],
        compiler_params=pltpu.CompilerParams(vmem_limit_bytes=4 << 20),
        name="merge",
    )(place, policy, stats)


def local(
    queries,
    key_rows,
    value_rows,
    out_weight,
    stream,
    final_gain,
    head_weight,
    token_ids,
    policy_logprob,
    doc_lengths,
    slab_start,
):
    ctx_count, tp_count = lax.axis_size("ctx"), lax.axis_size("tp")
    ctx, tp = lax.axis_index("ctx"), lax.axis_index("tp")
    chips = ctx_count // 2
    own_rows = queries.shape[0]
    blocks = ctx_count // tp_count
    mid = tp_count // 2
    place = jnp.stack([ctx, tp, slab_start[0]]).astype(jnp.int32)

    kv = [key_rows, value_rows, swap(key_rows, "ctx", 1), swap(value_rows, "ctx", 1)]
    kv = jnp.concatenate(kv, axis=1)
    kv, out_weight, stream = lax.optimization_barrier((kv, out_weight, stream))
    sets = list(zip(sides(queries, chips), sides(kv, chips)))
    if len(sets) < chips:
        half, inner = queries.shape[1] // 2, kv.shape[1] // 2
        below = jnp.concatenate([sets[2][0][:, :half], sets[2][1][:, :inner]], axis=1)
        above = jnp.concatenate([sets[1][0][:, half:], sets[1][1][:, inner:]], axis=1)
        sets.append((swap(below, "ctx", 2), swap(above, "ctx", 4)))
    out_sibling = swap(out_weight, "ctx", 1)
    stream_sibling = swap(stream, "ctx", 1)
    weight, mark = stage(place, out_weight, out_sibling, 1)
    mark, stream_sibling = lax.optimization_barrier((mark, stream_sibling))

    lens, kv_width = doc_lengths[None], key_rows.shape[1]
    far = attend(place, mark, lens, sets, kv_width, weight, range(mid, tp_count), tp_count, blocks)
    head_weight, *far = lax.optimization_barrier((head_weight, *far))
    head_sibling = swap(head_weight, "ctx", 1)
    near = attend(place, far[0], lens, sets, kv_width, weight, range(mid), tp_count, blocks)
    sums = [*near, *far]
    received = [swap(sums[k], "tp", k) for k in range(1, tp_count)]
    head_sibling, gain, tokens, sums[0] = lax.optimization_barrier((head_sibling, final_gain, token_ids, sums[0]))
    head, mark = stage(place, head_weight, head_sibling, ctx_count)
    gain, tokens = gain.astype(F32).reshape(ctx_count, -1), tokens[None]
    mark, gain, tokens = lax.optimization_barrier((mark, gain, tokens))
    updated = update(place, mark, stream, stream_sibling, [sums[0]] + received, blocks, own_rows)
    pieces, spans = [updated], []
    for k in range(1, tp_count):
        step = k & -k
        pieces.append(swap(pieces[k - step], "tp", step))
    for k, piece in enumerate(pieces):
        if k >= 2:
            piece, spans[k - 2] = lax.optimization_barrier((piece, spans[k - 2]))
        found = sides(piece, chips)
        spans.append(corners(found, k % 2))
    stats = score(place, tokens, gain, head, spans[:mid], 0, tp_count, own_rows, blocks) + score(
        place, tokens, gain, head, spans[mid:], mid, tp_count, own_rows, blocks
    )
    stats = lax.all_to_all(stats, ("ctx", "tp"), 0, 0, tiled=True)
    logprob, penalty = merge(place, policy_logprob[None], stats, chips, tp_count)
    return (logprob[0], penalty[0])


def solution(mesh):
    placed = (
        P("ctx", "tp"),
        P("ctx", "tp"),
        P("ctx", "tp"),
        P("tp", "ctx"),
        P("tp", "ctx"),
        P(),
        P(None, ("ctx", "tp")),
        P(),
        P("ctx"),
        P(),
        P(),
    )
    return jax.shard_map(
        local, mesh=mesh, in_specs=placed, out_specs=(P("ctx"), P("ctx")), check_vma=False
    )
```

```python
import jax
import jax.numpy as jnp
from jax import lax
from jax.experimental import pallas as pl
from jax.experimental.pallas import tpu as pltpu
from jax.sharding import PartitionSpec as P

HD = 128
EPSILON = 1e-06
CEILING = 10.0
NEGATIVE = -1e30
F32 = jnp.float32
BF16 = jnp.bfloat16
VMEM = pl.BlockSpec(memory_space=pltpu.VMEM)
SMEM = pl.BlockSpec(memory_space=pltpu.SMEM)
HBM = pl.BlockSpec(memory_space=pltpu.HBM)
ANY = pl.BlockSpec(memory_space=pl.ANY)


def swap(x, axis, k):
    size = lax.axis_size(axis)
    return lax.ppermute(x, axis, [(i, i ^ k) for i in range(size)])


def sides(piece, chips):
    if chips != 4:
        return [piece] + [swap(piece, "ctx", 2 * j) for j in range(1, chips)]
    return [piece, swap(piece, "ctx", 2), swap(piece, "ctx", 4)]


def corners(found, turn):
    if len(found) != 3:
        return found
    return [*found, swap(found[2 - turn], "ctx", 2 + 2 * turn)]


def attend_kernel(chips, tp_count, own_rows, kv_width, ks, blocks, place_ref, after_ref, lens_ref, weight_ref, *refs):
    outs = refs[2 * chips : 2 * chips + len(ks)]
    queries, keys, values, mixed = refs[2 * chips + len(ks) :]
    ctx, tp, slab_start = place_ref[0], place_ref[1], place_ref[2]
    kv_heads = kv_width // HD
    depth = queries.shape[1]
    group = depth // kv_width
    length = keys.shape[0]
    owners = [(tp ^ k) * blocks + 2 * b + lax.rem(ctx, 2) for k in ks for b in range(blocks // 2)]
    for j in range(chips):
        asked, kv = refs[2 * j], refs[2 * j + 1]
        own_at = pl.ds(pl.multiple_of((ctx ^ (2 * j)) * own_rows, own_rows), own_rows)
        sib_at = pl.ds(pl.multiple_of((ctx ^ (2 * j + 1)) * own_rows, own_rows), own_rows)
        for rows, first in ((own_at, 0), (sib_at, 2 * kv_width)):
            keys[rows, :] = kv[:, first : first + kv_width]
            values[rows, :] = kv[:, first + kv_width : first + 2 * kv_width]
        for i, owner in enumerate(owners):

            @pl.when(owner == (ctx ^ (2 * j)))
            def _(asked=asked, i=i):
                queries[i * own_rows : (i + 1) * own_rows, :] = asked[...]

    count = lens_ref.shape[1]
    first = lax.broadcasted_iota(jnp.int32, (count, count), 0)
    second = lax.broadcasted_iota(jnp.int32, (count, count), 1)
    column = jnp.sum(jnp.where(first == second, lens_ref[...], 0), axis=1, keepdims=True)
    ends = jnp.sum(jnp.where(first <= second, column, 0), axis=0, keepdims=True)
    columns = lax.broadcasted_iota(jnp.int32, (own_rows, length), 1)
    for i, owner in enumerate(owners):
        spot = owner * own_rows + lax.broadcasted_iota(jnp.int32, (own_rows, 1), 0)
        opened = jnp.max(jnp.where(ends <= spot + slab_start, ends, 0), axis=1, keepdims=True) - slab_start
        allowed = ((columns <= spot) & (columns >= opened))[None]
        at = slice(i * own_rows, (i + 1) * own_rows)
        for h in range(kv_heads):
            heads = [(h * group + g) * HD for g in range(group)]
            stack = jnp.concatenate([queries[at, head : head + HD] for head in heads], axis=0)
            scores = lax.dot_general(
                stack, keys[:, h * HD : (h + 1) * HD], (((1,), (1,)), ((), ())), preferred_element_type=F32
            ).reshape(group, own_rows, length)
            scores = jnp.where(allowed, scores, NEGATIVE)
            highest = jnp.max(scores, axis=2, keepdims=True)
            weights = jnp.exp((scores - highest) * HD ** (-0.5))
            denominator = jnp.sum(weights, axis=2, keepdims=True).reshape(group * own_rows, 1)
            mix = jnp.dot(
                weights.reshape(group * own_rows, length).astype(BF16),
                values[:, h * HD : (h + 1) * HD],
                preferred_element_type=F32,
            )
            mix = (mix / denominator).astype(BF16)
            for g, head in enumerate(heads):
                mixed[i * own_rows : (i + 1) * own_rows, head : head + HD] = mix[g * own_rows : (g + 1) * own_rows]
    product = jnp.dot(mixed[...], weight_ref[...], preferred_element_type=F32)
    span = blocks // 2 * own_rows
    for i, out in enumerate(outs):
        out[...] = product[i * span : (i + 1) * span].astype(out.dtype)


def attend(place, after, lens, sets, kv_width, weight, ks, tp_count, blocks):
    chips, own_rows = len(sets), sets[0][0].shape[0]
    length = 2 * chips * own_rows
    depth, width = weight.shape
    span = blocks // 2 * own_rows
    rows = len(ks) * span
    need = 2 * depth * width + chips * own_rows * depth * 2 + rows * (depth * 4 + width * 16) + 24 * 8 * own_rows * length
    return pl.pallas_call(
        lambda *refs: attend_kernel(chips, tp_count, own_rows, kv_width, ks, blocks, *refs),
        out_shape=[jax.ShapeDtypeStruct((span, width), F32 if k == 0 else BF16) for k in ks],
        in_specs=[SMEM, ANY] + [VMEM] * (2 + 2 * chips),
        out_specs=[VMEM] * len(ks),
        scratch_shapes=[
            pltpu.VMEM((rows, depth), BF16),
            pltpu.VMEM((length, kv_width), BF16),
            pltpu.VMEM((length, kv_width), BF16),
            pltpu.VMEM((rows, depth), BF16),
        ],
        compiler_params=pltpu.CompilerParams(vmem_limit_bytes=need + (8 << 20)),
        name="attend",
    )(place, after, lens, weight, *[part for one in sets for part in one])


def update_kernel(blocks, own_rows, place_ref, after_ref, stream_ref, stream_sib_ref, *refs):
    sums, out_ref, mark_ref = refs[:-2], refs[-2], refs[-1]
    mark_ref[...] = jnp.zeros(mark_ref.shape, F32)
    core = lax.rem(place_ref[0], 2)
    width = stream_ref.shape[1]
    for b in range(blocks // 2):
        source = pl.ds(pl.multiple_of((2 * b + core) * own_rows, own_rows), own_rows)
        target = slice(b * own_rows, (b + 1) * own_rows)
        for side, part in enumerate((stream_ref, stream_sib_ref)):
            columns = slice(side * width, (side + 1) * width)
            total = part[source, :].astype(F32)
            for one in sums:
                total += one[target, columns].astype(F32)
            out_ref[target, columns] = total.astype(BF16)


def update(place, after, stream, stream_sib, sums, blocks, own_rows):
    return pl.pallas_call(
        lambda *refs: update_kernel(blocks, own_rows, *refs),
        out_shape=[jax.ShapeDtypeStruct(sums[0].shape, BF16), jax.ShapeDtypeStruct((8, 128), F32)],
        in_specs=[SMEM, ANY] + [VMEM] * (2 + len(sums)),
        out_specs=[VMEM, VMEM],
        compiler_params=pltpu.CompilerParams(vmem_limit_bytes=6 << 20),
        name="update",
    )(place, after, stream, stream_sib, *sums)


def stage_kernel(place_ref, own_ref, sib_ref, both_ref, mark_ref, sems):
    ranks = sems.shape[1]
    part, width = own_ref.shape[0] // ranks, own_ref.shape[1]
    mark_ref[...] = jnp.zeros(mark_ref.shape, F32)
    if width % 128:
        for k in range(ranks):
            source = pl.ds(pl.multiple_of((place_ref[0] ^ k) * part, part), part) if ranks > 1 else slice(0, part)
            both_ref[k * part : (k + 1) * part, :width] = own_ref[source, :]
            both_ref[k * part : (k + 1) * part, width:] = sib_ref[source, :]
        return
    copies = []
    for k in range(ranks):
        source = pl.ds(pl.multiple_of((place_ref[0] ^ k) * part, part), part) if ranks > 1 else slice(0, part)
        target = slice(k * part, (k + 1) * part)
        copies.append(pltpu.make_async_copy(own_ref.at[source], both_ref.at[target, :width], sems.at[0, k]))
        copies.append(pltpu.make_async_copy(sib_ref.at[source], both_ref.at[target, width:], sems.at[1, k]))
    for copy in copies:
        copy.start()
    for copy in copies:
        copy.wait()


def stage(place, own, sib, ranks):
    depth, width = own.shape
    return pl.pallas_call(
        stage_kernel,
        out_shape=[jax.ShapeDtypeStruct((depth, 2 * width), BF16), jax.ShapeDtypeStruct((8, 128), F32)],
        in_specs=[SMEM] + [VMEM if width % 128 else HBM] * 2,
        out_specs=[VMEM, VMEM],
        scratch_shapes=[pltpu.SemaphoreType.DMA((2, ranks))],
        compiler_params=pltpu.CompilerParams(vmem_limit_bytes=(8 if width % 128 else 4) * depth * width + (4 << 20)),
        name="stage",
    )(place, own, sib)


def score_kernel(chips, tp_count, own_rows, blocks, first, place_ref, after_ref, ready_ref, tokens_ref, gain_ref, head_ref, *refs):
    pieces, out_ref, normed = refs[:-2], refs[-2], refs[-1]
    spans = len(pieces) // chips
    ctx, tp = place_ref[0], place_ref[1]
    ranks = 2 * chips
    part, vocab = head_ref.shape[0] // ranks, head_ref.shape[1] // 2
    span_rows = pieces[0].shape[0]
    squares = [jnp.zeros((span_rows, 1), F32)] * spans
    for j in range(chips):
        gain = jnp.concatenate([gain_ref[pl.ds(ctx ^ (2 * j), 1), :], gain_ref[pl.ds(ctx ^ (2 * j + 1), 1), :]], axis=1)
        for s in range(spans):
            wide = pieces[s * chips + j][...].astype(F32)
            squares[s] += jnp.sum(wide * wide, axis=1, keepdims=True)
            normed[s * span_rows : (s + 1) * span_rows, 2 * j * part : 2 * (j + 1) * part] = (wide * gain).astype(BF16)
    square = jnp.concatenate(squares, axis=0)
    inverse = lax.rsqrt(square * (1.0 / (ranks * part)) + EPSILON)
    logits = jnp.dot(normed[...], head_ref[...], preferred_element_type=F32) * inverse
    rows = logits.shape[0]
    column = lax.broadcasted_iota(jnp.int32, (1, 2 * vocab), 1)
    offset = jnp.where(column < vocab, (ctx * tp_count + tp) * vocab, ((ctx ^ 1) * tp_count + tp) * vocab - vocab)
    owners = [
        (tp ^ k) * blocks + 2 * b + lax.rem(ctx, 2) for k in range(first, first + spans) for b in range(blocks // 2)
    ]
    length = tokens_ref.shape[1]
    line = lax.broadcasted_iota(jnp.int32, (own_rows, length), 1) - lax.broadcasted_iota(jnp.int32, (own_rows, length), 0)
    tokens = jnp.concatenate(
        [
            jnp.sum(jnp.where(line == owner * own_rows, tokens_ref[...], 0), axis=1, keepdims=True)
            for owner in owners
        ],
        axis=0,
    )
    highest = jnp.max(logits, axis=1, keepdims=True)
    total = jnp.sum(jnp.exp(logits - highest), axis=1, keepdims=True)
    target = jnp.sum(jnp.where(column + offset == tokens, logits, 0.0), axis=1, keepdims=True)
    lane = lax.broadcasted_iota(jnp.int32, (rows, 128), 1)
    packed = jnp.where(lane == 0, highest, jnp.where(lane == 1, total, jnp.where(lane == 2, target, 0.0)))
    turned = packed.T[:8]
    out_ref[...] = jnp.zeros(out_ref.shape, F32)
    for i, owner in enumerate(owners):
        tile = turned[:, i * own_rows : (i + 1) * own_rows]
        for k in range(tp_count):
            out_ref[pl.ds(owner * tp_count + k, 1), :, :own_rows] = tile[None]


def score(place, after, ready, tokens, gain, head, spans, first, tp_count, own_rows, blocks):
    chips = len(spans[0])
    rows = len(spans) * spans[0][0].shape[0]
    depth, vocab = head.shape
    need = 2 * depth * vocab + rows * depth * 6 + rows * vocab * 4 * 8
    return pl.pallas_call(
        lambda *refs: score_kernel(chips, tp_count, own_rows, blocks, first, *refs),
        out_shape=jax.ShapeDtypeStruct((2 * chips * tp_count, 8, 128), F32),
        in_specs=[SMEM, ANY, ANY] + [VMEM] * (3 + len(spans) * chips),
        out_specs=VMEM,
        scratch_shapes=[pltpu.VMEM((rows, depth), BF16)],
        compiler_params=pltpu.CompilerParams(vmem_limit_bytes=need + (12 << 20)),
        name="score",
    )(place, after, ready, tokens, gain, head, *[piece for span in spans for piece in span])


def merge_kernel(chips, tp_count, place_ref, policy_ref, stats_ref, logprob_ref, penalty_ref):
    parity = lax.rem(place_ref[0], 2)
    own_rows = policy_ref.shape[1]
    tiles = [
        stats_ref[(2 * j + parity) * tp_count + k] for j in range(chips) for k in range(tp_count)
    ]
    highest = tiles[0][0:1]
    for tile in tiles[1:]:
        highest = jnp.maximum(highest, tile[0:1])
    total = jnp.zeros_like(highest)
    target = jnp.zeros_like(highest)
    for tile in tiles:
        total += tile[1:2] * jnp.exp(tile[0:1] - highest)
        target += tile[2:3]
    logprob = (target - (highest + jnp.log(total)))[:, :own_rows]
    ratio = logprob - policy_ref[...]
    logprob_ref[...] = logprob
    penalty_ref[...] = jnp.minimum(jnp.exp(ratio) - ratio - 1.0, CEILING)


def merge(place, policy, stats, chips, tp_count):
    shape = jax.ShapeDtypeStruct(policy.shape, F32)
    return pl.pallas_call(
        lambda *refs: merge_kernel(chips, tp_count, *refs),
        out_shape=[shape, shape],
        in_specs=[SMEM, VMEM, VMEM],
        out_specs=[VMEM, VMEM],
        compiler_params=pltpu.CompilerParams(vmem_limit_bytes=4 << 20),
        name="merge",
    )(place, policy, stats)


def local(
    queries,
    key_rows,
    value_rows,
    out_weight,
    stream,
    final_gain,
    head_weight,
    token_ids,
    policy_logprob,
    doc_lengths,
    slab_start,
):
    ctx_count, tp_count = lax.axis_size("ctx"), lax.axis_size("tp")
    ctx, tp = lax.axis_index("ctx"), lax.axis_index("tp")
    chips = ctx_count // 2
    own_rows = queries.shape[0]
    blocks = ctx_count // tp_count
    mid = tp_count // 2
    place = jnp.stack([ctx, tp, slab_start[0]]).astype(jnp.int32)

    asked = sides(queries, chips)
    kv = [key_rows, value_rows, swap(key_rows, "ctx", 1), swap(value_rows, "ctx", 1)]
    kv = jnp.concatenate(kv, axis=1)
    kv, out_weight, stream = lax.optimization_barrier((kv, out_weight, stream))
    out_sibling, stream_sibling = swap(out_weight, "ctx", 1), swap(stream, "ctx", 1)
    weight, mark = stage(place, out_weight, out_sibling, 1)
    later, mark = lax.optimization_barrier((kv, mark))
    around = [kv] + [swap(kv if j < 2 else later, "ctx", 2 * j) for j in range(1, 3 if chips == 4 else chips)]
    mark, stream_sibling = lax.optimization_barrier((mark, stream_sibling))
    sets = list(zip(corners(asked, 0), corners(around, 1)))

    lens, kv_width = doc_lengths[None], key_rows.shape[1]
    far = attend(place, mark, lens, sets, kv_width, weight, range(mid, tp_count), tp_count, blocks)
    head_weight, *far = lax.optimization_barrier((head_weight, *far))
    head_sibling = swap(head_weight, "ctx", 1)
    near = attend(place, far[0], lens, sets, kv_width, weight, range(mid), tp_count, blocks)
    sums = [*near, *far]
    received = [swap(sums[k], "tp", k) for k in range(1, tp_count)]
    gain, tokens, sums[0] = lax.optimization_barrier((final_gain, token_ids, sums[0]))
    gain, tokens = gain.astype(F32).reshape(ctx_count, -1), tokens[None]
    sums[0], gain, tokens, head_sibling = lax.optimization_barrier((sums[0], gain, tokens, head_sibling))
    updated, mark = update(place, sums[0], stream, stream_sibling, [sums[0]] + received, blocks, own_rows)
    here, mark, head_sibling = lax.optimization_barrier((updated, swap(mark, "ctx", 1), head_sibling))
    head, ready = stage(place, head_weight, head_sibling, ctx_count)
    pieces, spans = [updated], []
    for k in range(1, tp_count):
        step = k & -k
        if step < k:
            pieces[k - step], ready = lax.optimization_barrier((pieces[k - step], ready))
        pieces.append(swap(pieces[k - step], "tp", step))
    for k, piece in enumerate([here] + pieces[1:]):
        spans.append(sides(piece, chips))
    spans = [corners(span, k % 2) for k, span in enumerate(spans)]
    stats = score(place, mark, ready, tokens, gain, head, spans[:mid], 0, tp_count, own_rows, blocks) + score(
        place, mark, ready, tokens, gain, head, spans[mid:], mid, tp_count, own_rows, blocks
    )
    stats = lax.all_to_all(stats, ("ctx", "tp"), 0, 0, tiled=True)
    logprob, penalty = merge(place, policy_logprob[None], stats, chips, tp_count)
    return (logprob[0], penalty[0])


def solution(mesh):
    placed = (
        P("ctx", "tp"),
        P("ctx", "tp"),
        P("ctx", "tp"),
        P("tp", "ctx"),
        P("tp", "ctx"),
        P(),
        P(None, ("ctx", "tp")),
        P(),
        P("ctx"),
        P(),
        P(),
    )
    return jax.shard_map(
        local, mesh=mesh, in_specs=placed, out_specs=(P("ctx"), P("ctx")), check_vma=False
    )
```

```python
import jax
import jax.numpy as jnp
from jax import lax
from jax.experimental import pallas as pl
from jax.experimental.pallas import tpu as pltpu
from jax.sharding import PartitionSpec as P

HD = 128
LOG2E = 1.4426950408889634
EPSILON = 1e-06
CEILING = 10.0
NEGATIVE = -1e30
F32 = jnp.float32
BF16 = jnp.bfloat16
VMEM = pl.BlockSpec(memory_space=pltpu.VMEM)
SMEM = pl.BlockSpec(memory_space=pltpu.SMEM)
HBM = pl.BlockSpec(memory_space=pltpu.HBM)
ANY = pl.BlockSpec(memory_space=pl.ANY)


def swap(x, axis, k):
    size = lax.axis_size(axis)
    return lax.ppermute(x, axis, [(i, i ^ k) for i in range(size)])


def sides(piece, chips):
    if chips != 4:
        return [piece] + [swap(piece, "ctx", 2 * j) for j in range(1, chips)]
    far = swap(piece, "ctx", 4)
    return [piece, swap(piece, "ctx", 2), far]


def corners(found, turn):
    if len(found) != 3:
        return found
    return [*found, swap(found[2 - turn], "ctx", 2 + 2 * turn)]


def attend_kernel(chips, tp_count, own_rows, kv_width, ks, blocks, place_ref, after_ref, lens_ref, weight_ref, *refs):
    outs = refs[2 * chips : 2 * chips + len(ks)]
    queries, keys, values, mixed = refs[2 * chips + len(ks) :]
    ctx, tp, slab_start = place_ref[0], place_ref[1], place_ref[2]
    kv_heads = kv_width // HD
    depth = queries.shape[1]
    group = depth // kv_width
    length = keys.shape[0]
    owners = [(tp ^ k) * blocks + 2 * b + lax.rem(ctx, 2) for k in ks for b in range(blocks // 2)]
    half = depth // 2
    for h in range(kv_heads):
        values[:, (2 * h + 1) * HD : 2 * (h + 1) * HD] = jnp.ones((length, HD), BF16)
    for j in range(chips):
        low, high = refs[2 * j], refs[2 * j + 1]
        own_at = pl.ds(pl.multiple_of((ctx ^ (2 * j)) * own_rows, own_rows), own_rows)
        sib_at = pl.ds(pl.multiple_of((ctx ^ (2 * j + 1)) * own_rows, own_rows), own_rows)
        for rows, first in ((own_at, half), (sib_at, half + kv_width)):
            keys[rows, :] = low[:, first : first + kv_width]
            for h in range(kv_heads):
                values[rows, 2 * h * HD : (2 * h + 1) * HD] = high[:, first + h * HD : first + (h + 1) * HD]
        for i, owner in enumerate(owners):

            @pl.when(owner == (ctx ^ (2 * j)))
            def _(low=low, high=high, i=i):
                queries[i * own_rows : (i + 1) * own_rows, :half] = low[:, :half]
                queries[i * own_rows : (i + 1) * own_rows, half:] = high[:, :half]

    count = lens_ref.shape[1]
    first = lax.broadcasted_iota(jnp.int32, (count, count), 0)
    second = lax.broadcasted_iota(jnp.int32, (count, count), 1)
    column = jnp.sum(jnp.where(first == second, lens_ref[...], 0), axis=1, keepdims=True)
    ends = jnp.sum(jnp.where(first <= second, column, 0), axis=0, keepdims=True)
    columns = lax.broadcasted_iota(jnp.int32, (own_rows, length), 1)
    for i, owner in enumerate(owners):
        spot = owner * own_rows + lax.broadcasted_iota(jnp.int32, (own_rows, 1), 0)
        opened = jnp.max(jnp.where(ends <= spot + slab_start, ends, 0), axis=1, keepdims=True) - slab_start
        allowed = ((columns <= spot) & (columns >= opened))[None]
        at = slice(i * own_rows, (i + 1) * own_rows)
        for h in range(kv_heads):
            heads = [(h * group + g) * HD for g in range(group)]
            stack = jnp.concatenate([queries[at, head : head + HD] for head in heads], axis=0)
            scores = lax.dot_general(
                stack, keys[:, h * HD : (h + 1) * HD], (((1,), (1,)), ((), ())), preferred_element_type=F32
            ).reshape(group, own_rows, length)
            scores = jnp.where(allowed, scores, NEGATIVE)
            highest = jnp.max(scores, axis=2, keepdims=True)
            weights = jnp.exp2((scores - highest) * (HD ** (-0.5) * LOG2E))
            mix = jnp.dot(
                weights.reshape(group * own_rows, length).astype(BF16),
                values[:, 2 * h * HD : 2 * (h + 1) * HD],
                preferred_element_type=F32,
            )
            mix = (mix[:, :HD] / mix[:, HD:]).astype(BF16)
            for g, head in enumerate(heads):
                mixed[i * own_rows : (i + 1) * own_rows, head : head + HD] = mix[g * own_rows : (g + 1) * own_rows]
    product = jnp.dot(mixed[...], weight_ref[...], preferred_element_type=F32)
    span = blocks // 2 * own_rows
    for i, out in enumerate(outs):
        out[...] = product[i * span : (i + 1) * span].astype(out.dtype)


def attend(place, after, lens, sets, kv_width, weight, ks, tp_count, blocks):
    chips, own_rows = len(sets), sets[0][0].shape[0]
    length = 2 * chips * own_rows
    depth, width = weight.shape
    span = blocks // 2 * own_rows
    rows = len(ks) * span
    need = 2 * depth * width + chips * own_rows * depth * 2 + rows * (depth * 4 + width * 16) + 24 * 8 * own_rows * length
    return pl.pallas_call(
        lambda *refs: attend_kernel(chips, tp_count, own_rows, kv_width, ks, blocks, *refs),
        out_shape=[jax.ShapeDtypeStruct((span, width), F32 if k == 0 else BF16) for k in ks],
        in_specs=[SMEM, ANY] + [VMEM] * (2 + 2 * chips),
        out_specs=[VMEM] * len(ks),
        scratch_shapes=[
            pltpu.VMEM((rows, depth), BF16),
            pltpu.VMEM((length, kv_width), BF16),
            pltpu.VMEM((length, 2 * kv_width), BF16),
            pltpu.VMEM((rows, depth), BF16),
        ],
        compiler_params=pltpu.CompilerParams(vmem_limit_bytes=need + (8 << 20)),
        name="attend",
    )(place, after, lens, weight, *[part for one in sets for part in one])


def update_kernel(blocks, own_rows, place_ref, after_ref, stream_ref, stream_sib_ref, *refs):
    sums, out_ref, mark_ref = refs[:-2], refs[-2], refs[-1]
    mark_ref[...] = jnp.zeros(mark_ref.shape, F32)
    core = lax.rem(place_ref[0], 2)
    width = stream_ref.shape[1]
    for b in range(blocks // 2):
        source = pl.ds(pl.multiple_of((2 * b + core) * own_rows, own_rows), own_rows)
        target = slice(b * own_rows, (b + 1) * own_rows)
        for side, part in enumerate((stream_ref, stream_sib_ref)):
            columns = slice(side * width, (side + 1) * width)
            total = part[source, :].astype(F32)
            for one in sums:
                total += one[target, columns].astype(F32)
            out_ref[target, columns] = total.astype(BF16)


def update(place, after, stream, stream_sib, sums, blocks, own_rows):
    return pl.pallas_call(
        lambda *refs: update_kernel(blocks, own_rows, *refs),
        out_shape=[jax.ShapeDtypeStruct(sums[0].shape, BF16), jax.ShapeDtypeStruct((8, 128), F32)],
        in_specs=[SMEM, ANY] + [VMEM] * (2 + len(sums)),
        out_specs=[VMEM, VMEM],
        compiler_params=pltpu.CompilerParams(vmem_limit_bytes=6 << 20),
        name="update",
    )(place, after, stream, stream_sib, *sums)


def stage_kernel(place_ref, own_ref, sib_ref, both_ref, mark_ref, sems):
    ranks = sems.shape[1]
    part, width = own_ref.shape[0] // ranks, own_ref.shape[1]
    mark_ref[...] = jnp.zeros(mark_ref.shape, F32)
    if width % 128:
        for k in range(ranks):
            source = pl.ds(pl.multiple_of((place_ref[0] ^ k) * part, part), part) if ranks > 1 else slice(0, part)
            both_ref[k * part : (k + 1) * part, :width] = own_ref[source, :]
            both_ref[k * part : (k + 1) * part, width:] = sib_ref[source, :]
        return
    copies = []
    for k in range(ranks):
        source = pl.ds(pl.multiple_of((place_ref[0] ^ k) * part, part), part) if ranks > 1 else slice(0, part)
        target = slice(k * part, (k + 1) * part)
        copies.append(pltpu.make_async_copy(own_ref.at[source], both_ref.at[target, :width], sems.at[0, k]))
        copies.append(pltpu.make_async_copy(sib_ref.at[source], both_ref.at[target, width:], sems.at[1, k]))
    for copy in copies:
        copy.start()
    for copy in copies:
        copy.wait()


def stage(place, own, sib, ranks):
    depth, width = own.shape
    return pl.pallas_call(
        stage_kernel,
        out_shape=[jax.ShapeDtypeStruct((depth, 2 * width), BF16), jax.ShapeDtypeStruct((8, 128), F32)],
        in_specs=[SMEM] + [VMEM if width % 128 else HBM] * 2,
        out_specs=[VMEM, VMEM],
        scratch_shapes=[pltpu.SemaphoreType.DMA((2, ranks))],
        compiler_params=pltpu.CompilerParams(vmem_limit_bytes=(8 if width % 128 else 4) * depth * width + (4 << 20)),
        name="stage",
    )(place, own, sib)


def score_kernel(chips, tp_count, own_rows, blocks, first, place_ref, after_ref, ready_ref, tokens_ref, gain_ref, head_ref, *refs):
    pieces, out_ref, normed = refs[:-2], refs[-2], refs[-1]
    spans = len(pieces) // chips
    ctx, tp = place_ref[0], place_ref[1]
    ranks = 2 * chips
    part, vocab = head_ref.shape[0] // ranks, head_ref.shape[1] // 2
    span_rows = pieces[0].shape[0]
    squares = [jnp.zeros((span_rows, 1), F32)] * spans
    for j in range(chips):
        gain = jnp.concatenate([gain_ref[pl.ds(ctx ^ (2 * j), 1), :], gain_ref[pl.ds(ctx ^ (2 * j + 1), 1), :]], axis=1)
        for s in range(spans):
            wide = pieces[s * chips + j][...].astype(F32)
            squares[s] += jnp.sum(wide * wide, axis=1, keepdims=True)
            normed[s * span_rows : (s + 1) * span_rows, 2 * j * part : 2 * (j + 1) * part] = (wide * gain).astype(BF16)
    square = jnp.concatenate(squares, axis=0)
    inverse = lax.rsqrt(square * (1.0 / (ranks * part)) + EPSILON)
    logits = jnp.dot(normed[...], head_ref[...], preferred_element_type=F32) * inverse
    rows = logits.shape[0]
    column = lax.broadcasted_iota(jnp.int32, (1, 2 * vocab), 1)
    offset = jnp.where(column < vocab, (ctx * tp_count + tp) * vocab, ((ctx ^ 1) * tp_count + tp) * vocab - vocab)
    owners = [
        (tp ^ k) * blocks + 2 * b + lax.rem(ctx, 2) for k in range(first, first + spans) for b in range(blocks // 2)
    ]
    length = tokens_ref.shape[1]
    line = lax.broadcasted_iota(jnp.int32, (own_rows, length), 1) - lax.broadcasted_iota(jnp.int32, (own_rows, length), 0)
    tokens = jnp.concatenate(
        [
            jnp.sum(jnp.where(line == owner * own_rows, tokens_ref[...], 0), axis=1, keepdims=True)
            for owner in owners
        ],
        axis=0,
    )
    highest = jnp.max(logits, axis=1, keepdims=True)
    total = jnp.sum(jnp.exp(logits - highest), axis=1, keepdims=True)
    target = jnp.sum(jnp.where(column + offset == tokens, logits, 0.0), axis=1, keepdims=True)
    lane = lax.broadcasted_iota(jnp.int32, (rows, 128), 1)
    packed = jnp.where(lane == 0, highest, jnp.where(lane == 1, total, jnp.where(lane == 2, target, 0.0)))
    turned = packed.T[:8]
    out_ref[...] = jnp.zeros(out_ref.shape, F32)
    for i, owner in enumerate(owners):
        tile = turned[:, i * own_rows : (i + 1) * own_rows]
        for k in range(tp_count):
            out_ref[pl.ds(owner * tp_count + k, 1), :, :own_rows] = tile[None]


def score(place, after, ready, tokens, gain, head, spans, first, tp_count, own_rows, blocks):
    chips = len(spans[0])
    rows = len(spans) * spans[0][0].shape[0]
    depth, vocab = head.shape
    need = 2 * depth * vocab + rows * depth * 6 + rows * vocab * 4 * 8
    return pl.pallas_call(
        lambda *refs: score_kernel(chips, tp_count, own_rows, blocks, first, *refs),
        out_shape=jax.ShapeDtypeStruct((2 * chips * tp_count, 8, 128), F32),
        in_specs=[SMEM, ANY, ANY] + [VMEM] * (3 + len(spans) * chips),
        out_specs=VMEM,
        scratch_shapes=[pltpu.VMEM((rows, depth), BF16)],
        compiler_params=pltpu.CompilerParams(vmem_limit_bytes=need + (12 << 20)),
        name="score",
    )(place, after, ready, tokens, gain, head, *[piece for span in spans for piece in span])


def merge_kernel(chips, tp_count, place_ref, policy_ref, stats_ref, logprob_ref, penalty_ref):
    parity = lax.rem(place_ref[0], 2)
    own_rows = policy_ref.shape[1]
    tiles = [
        stats_ref[(2 * j + parity) * tp_count + k] for j in range(chips) for k in range(tp_count)
    ]
    highest = tiles[0][0:1]
    for tile in tiles[1:]:
        highest = jnp.maximum(highest, tile[0:1])
    total = jnp.zeros_like(highest)
    target = jnp.zeros_like(highest)
    for tile in tiles:
        total += tile[1:2] * jnp.exp(tile[0:1] - highest)
        target += tile[2:3]
    logprob = (target - (highest + jnp.log(total)))[:, :own_rows]
    ratio = logprob - policy_ref[...]
    logprob_ref[...] = logprob
    penalty_ref[...] = jnp.minimum(jnp.exp(ratio) - ratio - 1.0, CEILING)


def merge(place, policy, stats, chips, tp_count):
    shape = jax.ShapeDtypeStruct(policy.shape, F32)
    return pl.pallas_call(
        lambda *refs: merge_kernel(chips, tp_count, *refs),
        out_shape=[shape, shape],
        in_specs=[SMEM, VMEM, VMEM],
        out_specs=[VMEM, VMEM],
        compiler_params=pltpu.CompilerParams(vmem_limit_bytes=4 << 20),
        name="merge",
    )(place, policy, stats)


def local(
    queries,
    key_rows,
    value_rows,
    out_weight,
    stream,
    final_gain,
    head_weight,
    token_ids,
    policy_logprob,
    doc_lengths,
    slab_start,
):
    ctx_count, tp_count = lax.axis_size("ctx"), lax.axis_size("tp")
    ctx, tp = lax.axis_index("ctx"), lax.axis_index("tp")
    chips = ctx_count // 2
    own_rows = queries.shape[0]
    blocks = ctx_count // tp_count
    mid = tp_count // 2
    place = jnp.stack([ctx, tp, slab_start[0]]).astype(jnp.int32)

    half = queries.shape[1] // 2
    low = jnp.concatenate([queries[:, :half], key_rows, swap(key_rows, "ctx", 1)], axis=1)
    high = jnp.concatenate([queries[:, half:], value_rows, swap(value_rows, "ctx", 1)], axis=1)
    low, high, out_weight, stream = lax.optimization_barrier((low, high, out_weight, stream))
    sets = list(zip(corners(sides(low, chips), 0), corners(sides(high, chips), 1)))
    out_sibling, stream_sibling = swap(out_weight, "ctx", 1), swap(stream, "ctx", 1)
    weight, mark = stage(place, out_weight, out_sibling, 1)
    mark, stream_sibling = lax.optimization_barrier((mark, stream_sibling))

    lens, kv_width = doc_lengths[None], key_rows.shape[1]
    far = attend(place, mark, lens, sets, kv_width, weight, range(mid, tp_count), tp_count, blocks)
    head_weight, *far = lax.optimization_barrier((head_weight, *far))
    head_sibling = swap(head_weight, "ctx", 1)
    near = attend(place, far[0], lens, sets, kv_width, weight, range(mid), tp_count, blocks)
    sums = [*near, *far]
    received = [swap(sums[k], "tp", k) for k in range(1, tp_count)]
    gain, tokens, sums[0] = lax.optimization_barrier((final_gain, token_ids, sums[0]))
    gain, tokens = gain.astype(F32).reshape(ctx_count, -1), tokens[None]
    sums[0], gain, tokens, head_sibling = lax.optimization_barrier((sums[0], gain, tokens, head_sibling))
    updated, mark = update(place, sums[0], stream, stream_sibling, [sums[0]] + received, blocks, own_rows)
    here, mark, head_sibling = lax.optimization_barrier((updated, swap(mark, "ctx", 1), head_sibling))
    head, ready = stage(place, head_weight, head_sibling, ctx_count)
    pieces, spans = [updated], []
    for k in range(1, tp_count):
        step = k & -k
        if step < k:
            pieces[k - step], ready = lax.optimization_barrier((pieces[k - step], ready))
        pieces.append(swap(pieces[k - step], "tp", step))
    for k, piece in enumerate([here] + pieces[1:]):
        spans.append(sides(piece, chips))
    spans = [corners(span, k % 2) for k, span in enumerate(spans)]
    stats = score(place, mark, ready, tokens, gain, head, spans[:mid], 0, tp_count, own_rows, blocks) + score(
        place, mark, ready, tokens, gain, head, spans[mid:], mid, tp_count, own_rows, blocks
    )
    stats = lax.all_to_all(stats, ("ctx", "tp"), 0, 0, tiled=True)
    logprob, penalty = merge(place, policy_logprob[None], stats, chips, tp_count)
    return (logprob[0], penalty[0])


def solution(mesh):
    placed = (
        P("ctx", "tp"),
        P("ctx", "tp"),
        P("ctx", "tp"),
        P("tp", "ctx"),
        P("tp", "ctx"),
        P(),
        P(None, ("ctx", "tp")),
        P(),
        P("ctx"),
        P(),
        P(),
    )
    return jax.shard_map(
        local, mesh=mesh, in_specs=placed, out_specs=(P("ctx"), P("ctx")), check_vma=False
    )
```

```python
import jax
import jax.numpy as jnp
from jax import lax
from jax.experimental import pallas as pl
from jax.experimental.pallas import tpu as pltpu
from jax.sharding import PartitionSpec as P

HD = 128
LOG2E = 1.4426950408889634
EPSILON = 1e-06
CEILING = 10.0
NEGATIVE = -1e30
F32 = jnp.float32
BF16 = jnp.bfloat16
VMEM = pl.BlockSpec(memory_space=pltpu.VMEM)
SMEM = pl.BlockSpec(memory_space=pltpu.SMEM)
HBM = pl.BlockSpec(memory_space=pltpu.HBM)
ANY = pl.BlockSpec(memory_space=pl.ANY)


def swap(x, axis, k):
    size = lax.axis_size(axis)
    return lax.ppermute(x, axis, [(i, i ^ k) for i in range(size)])


def sides(piece, chips):
    if chips != 4:
        return [piece] + [swap(piece, "ctx", 2 * j) for j in range(1, chips)]
    far = swap(piece, "ctx", 4)
    return [piece, swap(piece, "ctx", 2), far]


def corners(found, turn):
    if len(found) != 3:
        return found
    return [*found, swap(found[2 - turn], "ctx", 2 + 2 * turn)]


def pack_kernel(all_ref, key_sib_ref, value_sib_ref, low_ref, high_ref):
    width = key_sib_ref.shape[1]
    half = (all_ref.shape[1] - 2 * width) // 2
    for side, (out_ref, sib_ref) in enumerate(((low_ref, key_sib_ref), (high_ref, value_sib_ref))):
        own = 2 * half + side * width
        out_ref[:, :half] = all_ref[:, side * half : (side + 1) * half]
        out_ref[:, half : half + width] = all_ref[:, own : own + width]
        out_ref[:, half + width :] = sib_ref[...]


def pack(together, key_sibling, value_sibling):
    rows, width = key_sibling.shape
    shape = jax.ShapeDtypeStruct((rows, together.shape[1] // 2 + width), BF16)
    return pl.pallas_call(
        pack_kernel,
        out_shape=[shape, shape],
        in_specs=[VMEM] * 3,
        out_specs=[VMEM, VMEM],
        compiler_params=pltpu.CompilerParams(vmem_limit_bytes=4 << 20),
        name="pack",
    )(together, key_sibling, value_sibling)


def attend_kernel(chips, tp_count, own_rows, kv_width, ks, blocks, place_ref, after_ref, lens_ref, weight_ref, *refs):
    outs = refs[2 * chips : 2 * chips + len(ks)]
    queries, keys, values, mixed = refs[2 * chips + len(ks) :]
    ctx, tp, slab_start = place_ref[0], place_ref[1], place_ref[2]
    kv_heads = kv_width // HD
    depth = queries.shape[1]
    group = depth // kv_width
    length = keys.shape[0]
    owners = [(tp ^ k) * blocks + 2 * b + lax.rem(ctx, 2) for k in ks for b in range(blocks // 2)]
    half = depth // 2
    for h in range(kv_heads):
        values[:, (2 * h + 1) * HD : 2 * (h + 1) * HD] = jnp.ones((length, HD), BF16)
    for j in range(chips):
        low, high = refs[2 * j], refs[2 * j + 1]
        own_at = pl.ds(pl.multiple_of((ctx ^ (2 * j)) * own_rows, own_rows), own_rows)
        sib_at = pl.ds(pl.multiple_of((ctx ^ (2 * j + 1)) * own_rows, own_rows), own_rows)
        for rows, first in ((own_at, half), (sib_at, half + kv_width)):
            keys[rows, :] = low[:, first : first + kv_width]
            for h in range(kv_heads):
                values[rows, 2 * h * HD : (2 * h + 1) * HD] = high[:, first + h * HD : first + (h + 1) * HD]
        for i, owner in enumerate(owners):

            @pl.when(owner == (ctx ^ (2 * j)))
            def _(low=low, high=high, i=i):
                queries[i * own_rows : (i + 1) * own_rows, :half] = low[:, :half]
                queries[i * own_rows : (i + 1) * own_rows, half:] = high[:, :half]

    count = lens_ref.shape[1]
    first = lax.broadcasted_iota(jnp.int32, (count, count), 0)
    second = lax.broadcasted_iota(jnp.int32, (count, count), 1)
    column = jnp.sum(jnp.where(first == second, lens_ref[...], 0), axis=1, keepdims=True)
    ends = jnp.sum(jnp.where(first <= second, column, 0), axis=0, keepdims=True)
    columns = lax.broadcasted_iota(jnp.int32, (own_rows, length), 1)
    for i, owner in enumerate(owners):
        spot = owner * own_rows + lax.broadcasted_iota(jnp.int32, (own_rows, 1), 0)
        opened = jnp.max(jnp.where(ends <= spot + slab_start, ends, 0), axis=1, keepdims=True) - slab_start
        allowed = ((columns <= spot) & (columns >= opened))[None]
        at = slice(i * own_rows, (i + 1) * own_rows)
        for h in range(kv_heads):
            heads = [(h * group + g) * HD for g in range(group)]
            stack = jnp.concatenate([queries[at, head : head + HD] for head in heads], axis=0)
            scores = lax.dot_general(
                stack, keys[:, h * HD : (h + 1) * HD], (((1,), (1,)), ((), ())), preferred_element_type=F32
            ).reshape(group, own_rows, length)
            scores = jnp.where(allowed, scores, NEGATIVE)
            highest = jnp.max(scores, axis=2, keepdims=True)
            weights = jnp.exp2((scores - highest) * (HD ** (-0.5) * LOG2E))
            mix = jnp.dot(
                weights.reshape(group * own_rows, length).astype(BF16),
                values[:, 2 * h * HD : 2 * (h + 1) * HD],
                preferred_element_type=F32,
            )
            mix = (mix[:, :HD] / mix[:, HD:]).astype(BF16)
            for g, head in enumerate(heads):
                mixed[i * own_rows : (i + 1) * own_rows, head : head + HD] = mix[g * own_rows : (g + 1) * own_rows]
    product = jnp.dot(mixed[...], weight_ref[...], preferred_element_type=F32)
    span = blocks // 2 * own_rows
    for i, out in enumerate(outs):
        out[...] = product[i * span : (i + 1) * span].astype(out.dtype)


def attend(place, after, lens, sets, kv_width, weight, ks, tp_count, blocks):
    chips, own_rows = len(sets), sets[0][0].shape[0]
    length = 2 * chips * own_rows
    depth, width = weight.shape
    span = blocks // 2 * own_rows
    rows = len(ks) * span
    need = 2 * depth * width + chips * own_rows * depth * 2 + rows * (depth * 4 + width * 16) + 24 * 8 * own_rows * length
    return pl.pallas_call(
        lambda *refs: attend_kernel(chips, tp_count, own_rows, kv_width, ks, blocks, *refs),
        out_shape=[jax.ShapeDtypeStruct((span, width), F32 if k == 0 else BF16) for k in ks],
        in_specs=[SMEM, ANY] + [VMEM] * (2 + 2 * chips),
        out_specs=[VMEM] * len(ks),
        scratch_shapes=[
            pltpu.VMEM((rows, depth), BF16),
            pltpu.VMEM((length, kv_width), BF16),
            pltpu.VMEM((length, 2 * kv_width), BF16),
            pltpu.VMEM((rows, depth), BF16),
        ],
        compiler_params=pltpu.CompilerParams(vmem_limit_bytes=need + (8 << 20)),
        name="attend",
    )(place, after, lens, weight, *[part for one in sets for part in one])


def update_kernel(blocks, own_rows, place_ref, after_ref, stream_ref, stream_sib_ref, *refs):
    sums, out_ref, mark_ref = refs[:-2], refs[-2], refs[-1]
    mark_ref[...] = jnp.zeros(mark_ref.shape, F32)
    core = lax.rem(place_ref[0], 2)
    width = stream_ref.shape[1]
    for b in range(blocks // 2):
        source = pl.ds(pl.multiple_of((2 * b + core) * own_rows, own_rows), own_rows)
        target = slice(b * own_rows, (b + 1) * own_rows)
        for side, part in enumerate((stream_ref, stream_sib_ref)):
            columns = slice(side * width, (side + 1) * width)
            total = part[source, :].astype(F32)
            for one in sums:
                total += one[target, columns].astype(F32)
            out_ref[target, columns] = total.astype(BF16)


def update(place, after, stream, stream_sib, sums, blocks, own_rows):
    return pl.pallas_call(
        lambda *refs: update_kernel(blocks, own_rows, *refs),
        out_shape=[jax.ShapeDtypeStruct(sums[0].shape, BF16), jax.ShapeDtypeStruct((8, 128), F32)],
        in_specs=[SMEM, ANY] + [VMEM] * (2 + len(sums)),
        out_specs=[VMEM, VMEM],
        compiler_params=pltpu.CompilerParams(vmem_limit_bytes=6 << 20),
        name="update",
    )(place, after, stream, stream_sib, *sums)


def stage_kernel(place_ref, own_ref, sib_ref, both_ref, mark_ref, sems):
    ranks = sems.shape[1]
    part, width = own_ref.shape[0] // ranks, own_ref.shape[1]
    mark_ref[...] = jnp.zeros(mark_ref.shape, F32)
    if width % 128:
        for k in range(ranks):
            source = pl.ds(pl.multiple_of((place_ref[0] ^ k) * part, part), part) if ranks > 1 else slice(0, part)
            both_ref[k * part : (k + 1) * part, :width] = own_ref[source, :]
            both_ref[k * part : (k + 1) * part, width:] = sib_ref[source, :]
        return
    copies = []
    for k in range(ranks):
        source = pl.ds(pl.multiple_of((place_ref[0] ^ k) * part, part), part) if ranks > 1 else slice(0, part)
        target = slice(k * part, (k + 1) * part)
        copies.append(pltpu.make_async_copy(own_ref.at[source], both_ref.at[target, :width], sems.at[0, k]))
        copies.append(pltpu.make_async_copy(sib_ref.at[source], both_ref.at[target, width:], sems.at[1, k]))
    for copy in copies:
        copy.start()
    for copy in copies:
        copy.wait()


def stage(place, own, sib, ranks):
    depth, width = own.shape
    return pl.pallas_call(
        stage_kernel,
        out_shape=[jax.ShapeDtypeStruct((depth, 2 * width), BF16), jax.ShapeDtypeStruct((8, 128), F32)],
        in_specs=[SMEM] + [VMEM if width % 128 else HBM] * 2,
        out_specs=[VMEM, VMEM],
        scratch_shapes=[pltpu.SemaphoreType.DMA((2, ranks))],
        compiler_params=pltpu.CompilerParams(vmem_limit_bytes=(8 if width % 128 else 4) * depth * width + (4 << 20)),
        name="stage",
    )(place, own, sib)


def score_kernel(chips, tp_count, own_rows, blocks, first, place_ref, after_ref, ready_ref, tokens_ref, gain_ref, head_ref, *refs):
    pieces, out_ref, normed = refs[:-2], refs[-2], refs[-1]
    if first:
        pieces, earlier_ref = pieces[:-1], pieces[-1]
    spans = len(pieces) // chips
    ctx, tp = place_ref[0], place_ref[1]
    ranks = 2 * chips
    part, vocab = head_ref.shape[0] // ranks, head_ref.shape[1] // 2
    span_rows = pieces[0].shape[0]
    squares = [jnp.zeros((span_rows, 1), F32)] * spans
    for j in range(chips):
        gain = jnp.concatenate([gain_ref[pl.ds(ctx ^ (2 * j), 1), :], gain_ref[pl.ds(ctx ^ (2 * j + 1), 1), :]], axis=1)
        for s in range(spans):
            wide = pieces[s * chips + j][...].astype(F32)
            squares[s] += jnp.sum(wide * wide, axis=1, keepdims=True)
            normed[s * span_rows : (s + 1) * span_rows, 2 * j * part : 2 * (j + 1) * part] = (wide * gain).astype(BF16)
    square = jnp.concatenate(squares, axis=0)
    inverse = lax.rsqrt(square * (1.0 / (ranks * part)) + EPSILON)
    logits = jnp.dot(normed[...], head_ref[...], preferred_element_type=F32) * inverse
    rows = logits.shape[0]
    column = lax.broadcasted_iota(jnp.int32, (1, 2 * vocab), 1)
    offset = jnp.where(column < vocab, (ctx * tp_count + tp) * vocab, ((ctx ^ 1) * tp_count + tp) * vocab - vocab)
    owners = [
        (tp ^ k) * blocks + 2 * b + lax.rem(ctx, 2) for k in range(first, first + spans) for b in range(blocks // 2)
    ]
    length = tokens_ref.shape[1]
    line = lax.broadcasted_iota(jnp.int32, (own_rows, length), 1) - lax.broadcasted_iota(jnp.int32, (own_rows, length), 0)
    tokens = jnp.concatenate(
        [
            jnp.sum(jnp.where(line == owner * own_rows, tokens_ref[...], 0), axis=1, keepdims=True)
            for owner in owners
        ],
        axis=0,
    )
    highest = jnp.max(logits, axis=1, keepdims=True)
    total = jnp.sum(jnp.exp(logits - highest), axis=1, keepdims=True)
    target = jnp.sum(jnp.where(column + offset == tokens, logits, 0.0), axis=1, keepdims=True)
    lane = lax.broadcasted_iota(jnp.int32, (rows, 128), 1)
    packed = jnp.where(lane == 0, highest, jnp.where(lane == 1, total, jnp.where(lane == 2, target, 0.0)))
    turned = packed.T[:8]
    out_ref[...] = earlier_ref[...] if first else jnp.zeros(out_ref.shape, F32)
    for i, owner in enumerate(owners):
        tile = turned[:, i * own_rows : (i + 1) * own_rows]
        for k in range(tp_count):
            out_ref[pl.ds(owner * tp_count + k, 1), :, :own_rows] = tile[None]


def score(place, after, ready, tokens, gain, head, spans, first, earlier, tp_count, own_rows, blocks):
    chips = len(spans[0])
    rows = len(spans) * spans[0][0].shape[0]
    depth, vocab = head.shape
    need = 2 * depth * vocab + rows * depth * 6 + rows * vocab * 4 * 8
    return pl.pallas_call(
        lambda *refs: score_kernel(chips, tp_count, own_rows, blocks, first, *refs),
        out_shape=jax.ShapeDtypeStruct((2 * chips * tp_count, 8, 128), F32),
        in_specs=[SMEM, ANY, ANY] + [VMEM] * (3 + len(spans) * chips + len(earlier)),
        out_specs=VMEM,
        scratch_shapes=[pltpu.VMEM((rows, depth), BF16)],
        compiler_params=pltpu.CompilerParams(vmem_limit_bytes=need + (12 << 20)),
        name="score",
    )(place, after, ready, tokens, gain, head, *[piece for span in spans for piece in span], *earlier)


def merge_kernel(chips, tp_count, place_ref, policy_ref, stats_ref, logprob_ref, penalty_ref):
    parity = lax.rem(place_ref[0], 2)
    own_rows = policy_ref.shape[1]
    tiles = [
        stats_ref[(2 * j + parity) * tp_count + k] for j in range(chips) for k in range(tp_count)
    ]
    highest = tiles[0][0:1]
    for tile in tiles[1:]:
        highest = jnp.maximum(highest, tile[0:1])
    total = jnp.zeros_like(highest)
    target = jnp.zeros_like(highest)
    for tile in tiles:
        total += tile[1:2] * jnp.exp(tile[0:1] - highest)
        target += tile[2:3]
    logprob = (target - (highest + jnp.log(total)))[:, :own_rows]
    ratio = logprob - policy_ref[...]
    logprob_ref[...] = logprob
    penalty_ref[...] = jnp.minimum(jnp.exp(ratio) - ratio - 1.0, CEILING)


def merge(place, policy, stats, chips, tp_count):
    shape = jax.ShapeDtypeStruct(policy.shape, F32)
    return pl.pallas_call(
        lambda *refs: merge_kernel(chips, tp_count, *refs),
        out_shape=[shape, shape],
        in_specs=[SMEM, VMEM, VMEM],
        out_specs=[VMEM, VMEM],
        compiler_params=pltpu.CompilerParams(vmem_limit_bytes=4 << 20),
        name="merge",
    )(place, policy, stats)


def local(
    queries,
    key_rows,
    value_rows,
    out_weight,
    stream,
    final_gain,
    head_weight,
    token_ids,
    policy_logprob,
    doc_lengths,
    slab_start,
):
    ctx_count, tp_count = lax.axis_size("ctx"), lax.axis_size("tp")
    ctx, tp = lax.axis_index("ctx"), lax.axis_index("tp")
    chips = ctx_count // 2
    own_rows = queries.shape[0]
    blocks = ctx_count // tp_count
    mid = tp_count // 2
    place = jnp.stack([ctx, tp, slab_start[0]]).astype(jnp.int32)

    together = jnp.concatenate([queries, key_rows, value_rows], axis=1)
    low, high = pack(together, swap(key_rows, "ctx", 1), swap(value_rows, "ctx", 1))
    low, high, out_weight, stream = lax.optimization_barrier((low, high, out_weight, stream))
    sets = list(zip(corners(sides(low, chips), 0), corners(sides(high, chips), 1)))
    out_sibling, stream_sibling = swap(out_weight, "ctx", 1), swap(stream, "ctx", 1)
    weight, mark = stage(place, out_weight, out_sibling, 1)
    mark, stream_sibling = lax.optimization_barrier((mark, stream_sibling))

    lens, kv_width = doc_lengths[None], key_rows.shape[1]
    far = attend(place, mark, lens, sets, kv_width, weight, range(mid, tp_count), tp_count, blocks)
    head_weight, *far = lax.optimization_barrier((head_weight, *far))
    head_sibling = swap(head_weight, "ctx", 1)
    near = attend(place, far[0], lens, sets, kv_width, weight, range(mid), tp_count, blocks)
    sums = [*near, *far]
    received = [swap(sums[k], "tp", k) for k in range(1, tp_count)]
    gain, tokens, sums[0] = lax.optimization_barrier((final_gain, token_ids, sums[0]))
    gain, tokens = gain.astype(F32).reshape(ctx_count, -1), tokens[None]
    sums[0], gain, tokens, head_sibling = lax.optimization_barrier((sums[0], gain, tokens, head_sibling))
    updated, mark = update(place, sums[0], stream, stream_sibling, [sums[0]] + received, blocks, own_rows)
    here, mark, head_sibling = lax.optimization_barrier((updated, swap(mark, "ctx", 1), head_sibling))
    head, ready = stage(place, head_weight, head_sibling, ctx_count)
    pieces, spans = [updated], []
    for k in range(1, tp_count):
        step = k & -k
        if step < k:
            pieces[k - step], ready = lax.optimization_barrier((pieces[k - step], ready))
        pieces.append(swap(pieces[k - step], "tp", step))
    for k, piece in enumerate([here] + pieces[1:]):
        if k == 1 and chips == 4:
            spans.append([piece] + [swap(one, "tp", 1) for one in spans[0][1:]])
        else:
            spans.append(sides(piece, chips))
    for k in range(tp_count):
        if k == 1 and chips == 4:
            spans[k].append(swap(spans[0][3], "tp", 1))
        else:
            spans[k] = corners(spans[k], k % 2)
    sizes = (tp_count, own_rows, blocks)
    stats = score(place, mark, ready, tokens, gain, head, spans[:mid], 0, [], *sizes)
    stats = score(place, mark, ready, tokens, gain, head, spans[mid:], mid, [stats], *sizes)
    stats = lax.all_to_all(stats, ("ctx", "tp"), 0, 0, tiled=True)
    logprob, penalty = merge(place, policy_logprob[None], stats, chips, tp_count)
    return (logprob[0], penalty[0])


def solution(mesh):
    placed = (
        P("ctx", "tp"),
        P("ctx", "tp"),
        P("ctx", "tp"),
        P("tp", "ctx"),
        P("tp", "ctx"),
        P(),
        P(None, ("ctx", "tp")),
        P(),
        P("ctx"),
        P(),
        P(),
    )
    return jax.shard_map(
        local, mesh=mesh, in_specs=placed, out_specs=(P("ctx"), P("ctx")), check_vma=False
    )
```

```python
import jax
import jax.numpy as jnp
from jax import lax
from jax.experimental import pallas as pl
from jax.experimental.pallas import tpu as pltpu
from jax.sharding import PartitionSpec as P

HD = 128
LOG2E = 1.4426950408889634
EPSILON = 1e-06
CEILING = 10.0
NEGATIVE = -1e30
F32 = jnp.float32
BF16 = jnp.bfloat16
VMEM = pl.BlockSpec(memory_space=pltpu.VMEM)
SMEM = pl.BlockSpec(memory_space=pltpu.SMEM)
HBM = pl.BlockSpec(memory_space=pltpu.HBM)
ANY = pl.BlockSpec(memory_space=pl.ANY)


def swap(x, axis, k):
    size = lax.axis_size(axis)
    return lax.ppermute(x, axis, [(i, i ^ k) for i in range(size)])


def sides(piece, chips):
    if chips != 4:
        return [piece] + [swap(piece, "ctx", 2 * j) for j in range(1, chips)]
    far = swap(piece, "ctx", 4)
    return [piece, swap(piece, "ctx", 2), far]


def corners(found, turn):
    if len(found) != 3:
        return found
    return [*found, swap(found[2 - turn], "ctx", 2 + 2 * turn)]


def pack_kernel(all_ref, key_sib_ref, value_sib_ref, low_ref, high_ref):
    width = key_sib_ref.shape[1]
    half = (all_ref.shape[1] - 2 * width) // 2
    for side, (out_ref, sib_ref) in enumerate(((low_ref, key_sib_ref), (high_ref, value_sib_ref))):
        own = 2 * half + side * width
        out_ref[:, :half] = all_ref[:, side * half : (side + 1) * half]
        out_ref[:, half : half + width] = all_ref[:, own : own + width]
        out_ref[:, half + width :] = sib_ref[...]


def pack(together, key_sibling, value_sibling):
    rows, width = key_sibling.shape
    shape = jax.ShapeDtypeStruct((rows, together.shape[1] // 2 + width), BF16)
    return pl.pallas_call(
        pack_kernel,
        out_shape=[shape, shape],
        in_specs=[VMEM] * 3,
        out_specs=[VMEM, VMEM],
        compiler_params=pltpu.CompilerParams(vmem_limit_bytes=4 << 20),
        name="pack",
    )(together, key_sibling, value_sibling)


def attend_kernel(chips, tp_count, own_rows, kv_width, ks, blocks, place_ref, after_ref, lens_ref, weight_ref, *refs):
    outs = refs[2 * chips : 2 * chips + len(ks)]
    queries, keys, values, mixed = refs[2 * chips + len(ks) :]
    ctx, tp, slab_start = place_ref[0], place_ref[1], place_ref[2]
    kv_heads = kv_width // HD
    depth = queries.shape[1]
    group = depth // kv_width
    length = keys.shape[0]
    owners = [(tp ^ k) * blocks + 2 * b + lax.rem(ctx, 2) for k in ks for b in range(blocks // 2)]
    half = depth // 2
    for h in range(kv_heads):
        values[:, (2 * h + 1) * HD : 2 * (h + 1) * HD] = jnp.ones((length, HD), BF16)
    for j in range(chips):
        low, high = refs[2 * j], refs[2 * j + 1]
        own_at = pl.ds(pl.multiple_of((ctx ^ (2 * j)) * own_rows, own_rows), own_rows)
        sib_at = pl.ds(pl.multiple_of((ctx ^ (2 * j + 1)) * own_rows, own_rows), own_rows)
        for rows, first in ((own_at, half), (sib_at, half + kv_width)):
            keys[rows, :] = low[:, first : first + kv_width]
            for h in range(kv_heads):
                values[rows, 2 * h * HD : (2 * h + 1) * HD] = high[:, first + h * HD : first + (h + 1) * HD]
        for i, owner in enumerate(owners):

            @pl.when(owner == (ctx ^ (2 * j)))
            def _(low=low, high=high, i=i):
                queries[i * own_rows : (i + 1) * own_rows, :half] = low[:, :half]
                queries[i * own_rows : (i + 1) * own_rows, half:] = high[:, :half]

    count = lens_ref.shape[1]
    first = lax.broadcasted_iota(jnp.int32, (count, count), 0)
    second = lax.broadcasted_iota(jnp.int32, (count, count), 1)
    column = jnp.sum(jnp.where(first == second, lens_ref[...], 0), axis=1, keepdims=True)
    ends = jnp.sum(jnp.where(first <= second, column, 0), axis=0, keepdims=True)
    columns = lax.broadcasted_iota(jnp.int32, (own_rows, length), 1)
    for i, owner in enumerate(owners):
        spot = owner * own_rows + lax.broadcasted_iota(jnp.int32, (own_rows, 1), 0)
        opened = jnp.max(jnp.where(ends <= spot + slab_start, ends, 0), axis=1, keepdims=True) - slab_start
        allowed = ((columns <= spot) & (columns >= opened))[None]
        at = slice(i * own_rows, (i + 1) * own_rows)
        for h in range(kv_heads):
            heads = [(h * group + g) * HD for g in range(group)]
            stack = jnp.concatenate([queries[at, head : head + HD] for head in heads], axis=0)
            scores = lax.dot_general(
                stack, keys[:, h * HD : (h + 1) * HD], (((1,), (1,)), ((), ())), preferred_element_type=F32
            ).reshape(group, own_rows, length)
            scores = jnp.where(allowed, scores, NEGATIVE)
            highest = jnp.max(scores, axis=2, keepdims=True)
            weights = jnp.exp2((scores - highest) * (HD ** (-0.5) * LOG2E))
            mix = jnp.dot(
                weights.reshape(group * own_rows, length).astype(BF16),
                values[:, 2 * h * HD : 2 * (h + 1) * HD],
                preferred_element_type=F32,
            )
            mix = (mix[:, :HD] / mix[:, HD:]).astype(BF16)
            for g, head in enumerate(heads):
                mixed[i * own_rows : (i + 1) * own_rows, head : head + HD] = mix[g * own_rows : (g + 1) * own_rows]
    product = jnp.dot(mixed[...], weight_ref[...], preferred_element_type=F32)
    span = blocks // 2 * own_rows
    for i, out in enumerate(outs):
        out[...] = product[i * span : (i + 1) * span].astype(out.dtype)


def attend(place, after, lens, sets, kv_width, weight, ks, tp_count, blocks):
    chips, own_rows = len(sets), sets[0][0].shape[0]
    length = 2 * chips * own_rows
    depth, width = weight.shape
    span = blocks // 2 * own_rows
    rows = len(ks) * span
    need = 2 * depth * width + chips * own_rows * depth * 2 + rows * (depth * 4 + width * 16) + 24 * 8 * own_rows * length
    return pl.pallas_call(
        lambda *refs: attend_kernel(chips, tp_count, own_rows, kv_width, ks, blocks, *refs),
        out_shape=[jax.ShapeDtypeStruct((span, width), F32 if k == 0 else BF16) for k in ks],
        in_specs=[SMEM, ANY] + [VMEM] * (2 + 2 * chips),
        out_specs=[VMEM] * len(ks),
        scratch_shapes=[
            pltpu.VMEM((rows, depth), BF16),
            pltpu.VMEM((length, kv_width), BF16),
            pltpu.VMEM((length, 2 * kv_width), BF16),
            pltpu.VMEM((rows, depth), BF16),
        ],
        compiler_params=pltpu.CompilerParams(vmem_limit_bytes=need + (8 << 20)),
        name="attend",
    )(place, after, lens, weight, *[part for one in sets for part in one])


def update_kernel(blocks, own_rows, place_ref, after_ref, stream_ref, stream_sib_ref, *refs):
    sums, out_ref, mark_ref = refs[:-2], refs[-2], refs[-1]
    mark_ref[...] = jnp.zeros(mark_ref.shape, F32)
    core = lax.rem(place_ref[0], 2)
    width = stream_ref.shape[1]
    for b in range(blocks // 2):
        source = pl.ds(pl.multiple_of((2 * b + core) * own_rows, own_rows), own_rows)
        target = slice(b * own_rows, (b + 1) * own_rows)
        for side, part in enumerate((stream_ref, stream_sib_ref)):
            columns = slice(side * width, (side + 1) * width)
            total = part[source, :].astype(F32)
            for one in sums:
                total += one[target, columns].astype(F32)
            out_ref[target, columns] = total.astype(BF16)


def update(place, after, stream, stream_sib, sums, blocks, own_rows):
    return pl.pallas_call(
        lambda *refs: update_kernel(blocks, own_rows, *refs),
        out_shape=[jax.ShapeDtypeStruct(sums[0].shape, BF16), jax.ShapeDtypeStruct((8, 128), F32)],
        in_specs=[SMEM, ANY] + [VMEM] * (2 + len(sums)),
        out_specs=[VMEM, VMEM],
        compiler_params=pltpu.CompilerParams(vmem_limit_bytes=6 << 20),
        name="update",
    )(place, after, stream, stream_sib, *sums)


def stage_kernel(place_ref, own_ref, sib_ref, both_ref, mark_ref, sems):
    ranks = sems.shape[1]
    part, width = own_ref.shape[0] // ranks, own_ref.shape[1]
    mark_ref[...] = jnp.zeros(mark_ref.shape, F32)
    if width % 128:
        for k in range(ranks):
            source = pl.ds(pl.multiple_of((place_ref[0] ^ k) * part, part), part) if ranks > 1 else slice(0, part)
            both_ref[k * part : (k + 1) * part, :width] = own_ref[source, :]
            both_ref[k * part : (k + 1) * part, width:] = sib_ref[source, :]
        return
    copies = []
    for k in range(ranks):
        source = pl.ds(pl.multiple_of((place_ref[0] ^ k) * part, part), part) if ranks > 1 else slice(0, part)
        target = slice(k * part, (k + 1) * part)
        copies.append(pltpu.make_async_copy(own_ref.at[source], both_ref.at[target, :width], sems.at[0, k]))
        copies.append(pltpu.make_async_copy(sib_ref.at[source], both_ref.at[target, width:], sems.at[1, k]))
    for copy in copies:
        copy.start()
    for copy in copies:
        copy.wait()


def stage(place, own, sib, ranks):
    depth, width = own.shape
    return pl.pallas_call(
        stage_kernel,
        out_shape=[jax.ShapeDtypeStruct((depth, 2 * width), BF16), jax.ShapeDtypeStruct((8, 128), F32)],
        in_specs=[SMEM] + [VMEM if width % 128 else HBM] * 2,
        out_specs=[VMEM, VMEM],
        scratch_shapes=[pltpu.SemaphoreType.DMA((2, ranks))],
        compiler_params=pltpu.CompilerParams(vmem_limit_bytes=(8 if width % 128 else 4) * depth * width + (4 << 20)),
        name="stage",
    )(place, own, sib)


def score_kernel(chips, tp_count, own_rows, blocks, first, place_ref, after_ref, ready_ref, tokens_ref, gain_ref, head_ref, *refs):
    pieces, out_ref, normed = refs[:-2], refs[-2], refs[-1]
    if first:
        pieces, earlier_ref = pieces[:-1], pieces[-1]
    spans = len(pieces) // chips
    ctx, tp = place_ref[0], place_ref[1]
    ranks = 2 * chips
    part, vocab = head_ref.shape[0] // ranks, head_ref.shape[1] // 2
    span_rows = pieces[0].shape[0]
    squares = [jnp.zeros((span_rows, 1), F32)] * spans
    for j in range(chips):
        gain = jnp.concatenate([gain_ref[pl.ds(ctx ^ (2 * j), 1), :], gain_ref[pl.ds(ctx ^ (2 * j + 1), 1), :]], axis=1)
        for s in range(spans):
            wide = pieces[s * chips + j][...].astype(F32)
            squares[s] += jnp.sum(wide * wide, axis=1, keepdims=True)
            normed[s * span_rows : (s + 1) * span_rows, 2 * j * part : 2 * (j + 1) * part] = (wide * gain).astype(BF16)
    square = jnp.concatenate(squares, axis=0)
    inverse = lax.rsqrt(square * (1.0 / (ranks * part)) + EPSILON)
    logits = jnp.dot(normed[...], head_ref[...], preferred_element_type=F32) * inverse
    rows = logits.shape[0]
    column = lax.broadcasted_iota(jnp.int32, (1, 2 * vocab), 1)
    offset = jnp.where(column < vocab, (ctx * tp_count + tp) * vocab, ((ctx ^ 1) * tp_count + tp) * vocab - vocab)
    owners = [
        (tp ^ k) * blocks + 2 * b + lax.rem(ctx, 2) for k in range(first, first + spans) for b in range(blocks // 2)
    ]
    length = tokens_ref.shape[1]
    line = lax.broadcasted_iota(jnp.int32, (own_rows, length), 1) - lax.broadcasted_iota(jnp.int32, (own_rows, length), 0)
    tokens = jnp.concatenate(
        [
            jnp.sum(jnp.where(line == owner * own_rows, tokens_ref[...], 0), axis=1, keepdims=True)
            for owner in owners
        ],
        axis=0,
    )
    highest = jnp.max(logits, axis=1, keepdims=True)
    total = jnp.sum(jnp.exp(logits - highest), axis=1, keepdims=True)
    target = jnp.sum(jnp.where(column + offset == tokens, logits, 0.0), axis=1, keepdims=True)
    lane = lax.broadcasted_iota(jnp.int32, (rows, 128), 1)
    packed = jnp.where(lane == 0, highest, jnp.where(lane == 1, total, jnp.where(lane == 2, target, 0.0)))
    turned = packed.T[:4]
    out_ref[...] = earlier_ref[...] if first else jnp.zeros(out_ref.shape, F32)
    for i, owner in enumerate(owners):
        tile = turned[:, i * own_rows : (i + 1) * own_rows]
        for k in range(tp_count):
            out_ref[pl.ds(owner * tp_count + k, 1), :, :own_rows] = tile[None]


def score(place, after, ready, tokens, gain, head, spans, first, earlier, tp_count, own_rows, blocks):
    chips = len(spans[0])
    rows = len(spans) * spans[0][0].shape[0]
    depth, vocab = head.shape
    need = 2 * depth * vocab + rows * depth * 6 + rows * vocab * 4 * 8
    return pl.pallas_call(
        lambda *refs: score_kernel(chips, tp_count, own_rows, blocks, first, *refs),
        out_shape=jax.ShapeDtypeStruct((2 * chips * tp_count, 4, 128), F32),
        in_specs=[SMEM, ANY, ANY] + [VMEM] * (3 + len(spans) * chips + len(earlier)),
        out_specs=VMEM,
        scratch_shapes=[pltpu.VMEM((rows, depth), BF16)],
        compiler_params=pltpu.CompilerParams(vmem_limit_bytes=need + (12 << 20)),
        name="score",
    )(place, after, ready, tokens, gain, head, *[piece for span in spans for piece in span], *earlier)


def merge_kernel(chips, tp_count, place_ref, policy_ref, stats_ref, logprob_ref, penalty_ref):
    parity = lax.rem(place_ref[0], 2)
    own_rows = policy_ref.shape[1]
    tiles = [
        stats_ref[(2 * j + parity) * tp_count + k] for j in range(chips) for k in range(tp_count)
    ]
    highest = tiles[0][0:1]
    for tile in tiles[1:]:
        highest = jnp.maximum(highest, tile[0:1])
    total = jnp.zeros_like(highest)
    target = jnp.zeros_like(highest)
    for tile in tiles:
        total += tile[1:2] * jnp.exp(tile[0:1] - highest)
        target += tile[2:3]
    logprob = (target - (highest + jnp.log(total)))[:, :own_rows]
    ratio = logprob - policy_ref[...]
    logprob_ref[...] = logprob
    penalty_ref[...] = jnp.minimum(jnp.exp(ratio) - ratio - 1.0, CEILING)


def merge(place, policy, stats, chips, tp_count):
    shape = jax.ShapeDtypeStruct(policy.shape, F32)
    return pl.pallas_call(
        lambda *refs: merge_kernel(chips, tp_count, *refs),
        out_shape=[shape, shape],
        in_specs=[SMEM, VMEM, VMEM],
        out_specs=[VMEM, VMEM],
        compiler_params=pltpu.CompilerParams(vmem_limit_bytes=4 << 20),
        name="merge",
    )(place, policy, stats)


def local(
    queries,
    key_rows,
    value_rows,
    out_weight,
    stream,
    final_gain,
    head_weight,
    token_ids,
    policy_logprob,
    doc_lengths,
    slab_start,
):
    ctx_count, tp_count = lax.axis_size("ctx"), lax.axis_size("tp")
    ctx, tp = lax.axis_index("ctx"), lax.axis_index("tp")
    chips = ctx_count // 2
    own_rows = queries.shape[0]
    blocks = ctx_count // tp_count
    mid = tp_count // 2
    place = jnp.stack([ctx, tp, slab_start[0]]).astype(jnp.int32)

    together = jnp.concatenate([queries, key_rows, value_rows], axis=1)
    low, high = pack(together, swap(key_rows, "ctx", 1), swap(value_rows, "ctx", 1))
    low, high, out_weight, stream = lax.optimization_barrier((low, high, out_weight, stream))
    sets = list(zip(corners(sides(low, chips), 0), corners(sides(high, chips), 1)))
    out_sibling, stream_sibling = swap(out_weight, "ctx", 1), swap(stream, "ctx", 1)
    weight, mark = stage(place, out_weight, out_sibling, 1)
    mark, stream_sibling = lax.optimization_barrier((mark, stream_sibling))

    lens, kv_width = doc_lengths[None], key_rows.shape[1]
    far = attend(place, mark, lens, sets, kv_width, weight, range(mid, tp_count), tp_count, blocks)
    head_weight, *far = lax.optimization_barrier((head_weight, *far))
    head_sibling = swap(head_weight, "ctx", 1)
    near = attend(place, far[0], lens, sets, kv_width, weight, range(mid), tp_count, blocks)
    sums = [*near, *far]
    received = [swap(sums[k], "tp", k) for k in range(1, tp_count)]
    gain, tokens, sums[0] = lax.optimization_barrier((final_gain, token_ids, sums[0]))
    gain, tokens = gain.astype(F32).reshape(ctx_count, -1), tokens[None]
    sums[0], gain, tokens, head_sibling = lax.optimization_barrier((sums[0], gain, tokens, head_sibling))
    updated, mark = update(place, sums[0], stream, stream_sibling, [sums[0]] + received, blocks, own_rows)
    here, mark, head_sibling = lax.optimization_barrier((updated, swap(mark, "ctx", 1), head_sibling))
    head, ready = stage(place, head_weight, head_sibling, ctx_count)
    pieces, spans = [updated], []
    for k in range(1, tp_count):
        step = k & -k
        if step < k:
            pieces[k - step], ready = lax.optimization_barrier((pieces[k - step], ready))
        pieces.append(swap(pieces[k - step], "tp", step))
    for k, piece in enumerate([here] + pieces[1:]):
        if k == 1 and chips == 4:
            spans.append([piece] + [swap(one, "tp", 1) for one in spans[0][1:]])
        else:
            spans.append(sides(piece, chips))
    for k in range(tp_count):
        if k == 1 and chips == 4:
            spans[k].append(swap(spans[0][3], "tp", 1))
        else:
            spans[k] = corners(spans[k], k % 2)
    sizes = (tp_count, own_rows, blocks)
    stats = score(place, mark, ready, tokens, gain, head, spans[:mid], 0, [], *sizes)
    stats = score(place, mark, ready, tokens, gain, head, spans[mid:], mid, [stats], *sizes)
    stats = lax.all_to_all(stats, ("ctx", "tp"), 0, 0, tiled=True)
    logprob, penalty = merge(place, policy_logprob[None], stats, chips, tp_count)
    return (logprob[0], penalty[0])


def solution(mesh):
    placed = (
        P("ctx", "tp"),
        P("ctx", "tp"),
        P("ctx", "tp"),
        P("tp", "ctx"),
        P("tp", "ctx"),
        P(),
        P(None, ("ctx", "tp")),
        P(),
        P("ctx"),
        P(),
        P(),
    )
    return jax.shard_map(
        local, mesh=mesh, in_specs=placed, out_specs=(P("ctx"), P("ctx")), check_vma=False
    )
```

```python
import jax
import jax.numpy as jnp
from jax import lax
from jax.experimental import pallas as pl
from jax.experimental.pallas import tpu as pltpu
from jax.sharding import PartitionSpec as P

HD = 128
LOG2E = 1.4426950408889634
EPSILON = 1e-06
CEILING = 10.0
NEGATIVE = -1e30
F32 = jnp.float32
BF16 = jnp.bfloat16
VMEM = pl.BlockSpec(memory_space=pltpu.VMEM)
SMEM = pl.BlockSpec(memory_space=pltpu.SMEM)
HBM = pl.BlockSpec(memory_space=pltpu.HBM)
ANY = pl.BlockSpec(memory_space=pl.ANY)


def swap(x, axis, k):
    size = lax.axis_size(axis)
    return lax.ppermute(x, axis, [(i, i ^ k) for i in range(size)])


def sides(piece, chips):
    if chips != 4:
        return [piece] + [swap(piece, "ctx", 2 * j) for j in range(1, chips)]
    far = swap(piece, "ctx", 4)
    return [piece, swap(piece, "ctx", 2), far]


def corners(found, turn):
    if len(found) != 3:
        return found
    return [*found, swap(found[2 - turn], "ctx", 2 + 2 * turn)]


def pack_kernel(all_ref, key_sib_ref, value_sib_ref, low_ref, high_ref):
    width = key_sib_ref.shape[1]
    half = (all_ref.shape[1] - 2 * width) // 2
    for side, (out_ref, sib_ref) in enumerate(((low_ref, key_sib_ref), (high_ref, value_sib_ref))):
        own = 2 * half + side * width
        out_ref[:, :half] = all_ref[:, side * half : (side + 1) * half]
        out_ref[:, half : half + width] = all_ref[:, own : own + width]
        out_ref[:, half + width :] = sib_ref[...]


def pack(together, key_sibling, value_sibling):
    rows, width = key_sibling.shape
    shape = jax.ShapeDtypeStruct((rows, together.shape[1] // 2 + width), BF16)
    return pl.pallas_call(
        pack_kernel,
        out_shape=[shape, shape],
        in_specs=[VMEM] * 3,
        out_specs=[VMEM, VMEM],
        compiler_params=pltpu.CompilerParams(vmem_limit_bytes=4 << 20),
        name="pack",
    )(together, key_sibling, value_sibling)


def attend_kernel(chips, tp_count, own_rows, kv_width, ks, blocks, place_ref, after_ref, lens_ref, weight_ref, *refs):
    outs = refs[2 * chips : 2 * chips + len(ks)]
    queries, keys, values, mixed = refs[2 * chips + len(ks) :]
    ctx, tp, slab_start = place_ref[0], place_ref[1], place_ref[2]
    kv_heads = kv_width // HD
    depth = queries.shape[1]
    group = depth // kv_width
    length = keys.shape[0]
    owners = [(tp ^ k) * blocks + 2 * b + lax.rem(ctx, 2) for k in ks for b in range(blocks // 2)]
    half = depth // 2
    for h in range(kv_heads):
        values[:, (2 * h + 1) * HD : 2 * (h + 1) * HD] = jnp.ones((length, HD), BF16)
    for j in range(chips):
        low, high = refs[2 * j], refs[2 * j + 1]
        own_at = pl.ds(pl.multiple_of((ctx ^ (2 * j)) * own_rows, own_rows), own_rows)
        sib_at = pl.ds(pl.multiple_of((ctx ^ (2 * j + 1)) * own_rows, own_rows), own_rows)
        for rows, first in ((own_at, half), (sib_at, half + kv_width)):
            keys[rows, :] = low[:, first : first + kv_width]
            for h in range(kv_heads):
                values[rows, 2 * h * HD : (2 * h + 1) * HD] = high[:, first + h * HD : first + (h + 1) * HD]
        for i, owner in enumerate(owners):

            @pl.when(owner == (ctx ^ (2 * j)))
            def _(low=low, high=high, i=i):
                queries[i * own_rows : (i + 1) * own_rows, :half] = low[:, :half]
                queries[i * own_rows : (i + 1) * own_rows, half:] = high[:, :half]

    count = lens_ref.shape[1]
    first = lax.broadcasted_iota(jnp.int32, (count, count), 0)
    second = lax.broadcasted_iota(jnp.int32, (count, count), 1)
    column = jnp.sum(jnp.where(first == second, lens_ref[...], 0), axis=1, keepdims=True)
    ends = jnp.sum(jnp.where(first <= second, column, 0), axis=0, keepdims=True)
    columns = lax.broadcasted_iota(jnp.int32, (own_rows, length), 1)
    for i, owner in enumerate(owners):
        spot = owner * own_rows + lax.broadcasted_iota(jnp.int32, (own_rows, 1), 0)
        opened = jnp.max(jnp.where(ends <= spot + slab_start, ends, 0), axis=1, keepdims=True) - slab_start
        allowed = ((columns <= spot) & (columns >= opened))[None]
        at = slice(i * own_rows, (i + 1) * own_rows)
        for h in range(kv_heads):
            heads = [(h * group + g) * HD for g in range(group)]
            stack = jnp.concatenate([queries[at, head : head + HD] for head in heads], axis=0)
            scores = lax.dot_general(
                stack, keys[:, h * HD : (h + 1) * HD], (((1,), (1,)), ((), ())), preferred_element_type=F32
            ).reshape(group, own_rows, length)
            scores = jnp.where(allowed, scores, NEGATIVE)
            highest = jnp.max(scores, axis=2, keepdims=True)
            weights = jnp.exp2((scores - highest) * (HD ** (-0.5) * LOG2E))
            mix = jnp.dot(
                weights.reshape(group * own_rows, length).astype(BF16),
                values[:, 2 * h * HD : 2 * (h + 1) * HD],
                preferred_element_type=F32,
            )
            mix = (mix[:, :HD] / mix[:, HD:]).astype(BF16)
            for g, head in enumerate(heads):
                mixed[i * own_rows : (i + 1) * own_rows, head : head + HD] = mix[g * own_rows : (g + 1) * own_rows]
    product = jnp.dot(mixed[...], weight_ref[...], preferred_element_type=F32)
    span = blocks // 2 * own_rows
    for i, out in enumerate(outs):
        out[...] = product[i * span : (i + 1) * span].astype(out.dtype)


def attend(place, after, lens, sets, kv_width, weight, ks, tp_count, blocks):
    chips, own_rows = len(sets), sets[0][0].shape[0]
    length = 2 * chips * own_rows
    depth, width = weight.shape
    span = blocks // 2 * own_rows
    rows = len(ks) * span
    need = 2 * depth * width + chips * own_rows * depth * 2 + rows * (depth * 4 + width * 16) + 24 * 8 * own_rows * length
    return pl.pallas_call(
        lambda *refs: attend_kernel(chips, tp_count, own_rows, kv_width, ks, blocks, *refs),
        out_shape=[jax.ShapeDtypeStruct((span, width), F32 if k == 0 else BF16) for k in ks],
        in_specs=[SMEM, ANY] + [VMEM] * (2 + 2 * chips),
        out_specs=[VMEM] * len(ks),
        scratch_shapes=[
            pltpu.VMEM((rows, depth), BF16),
            pltpu.VMEM((length, kv_width), BF16),
            pltpu.VMEM((length, 2 * kv_width), BF16),
            pltpu.VMEM((rows, depth), BF16),
        ],
        compiler_params=pltpu.CompilerParams(vmem_limit_bytes=need + (8 << 20)),
        name="attend",
    )(place, after, lens, weight, *[part for one in sets for part in one])


def update_kernel(blocks, own_rows, place_ref, after_ref, stream_ref, stream_sib_ref, *refs):
    sums, out_ref, mark_ref = refs[:-2], refs[-2], refs[-1]
    mark_ref[...] = jnp.zeros(mark_ref.shape, F32)
    core = lax.rem(place_ref[0], 2)
    width = stream_ref.shape[1]
    for b in range(blocks // 2):
        source = pl.ds(pl.multiple_of((2 * b + core) * own_rows, own_rows), own_rows)
        target = slice(b * own_rows, (b + 1) * own_rows)
        for side, part in enumerate((stream_ref, stream_sib_ref)):
            columns = slice(side * width, (side + 1) * width)
            total = part[source, :].astype(F32)
            for one in sums:
                total += one[target, columns].astype(F32)
            out_ref[target, columns] = total.astype(BF16)


def update(place, after, stream, stream_sib, sums, blocks, own_rows):
    return pl.pallas_call(
        lambda *refs: update_kernel(blocks, own_rows, *refs),
        out_shape=[jax.ShapeDtypeStruct(sums[0].shape, BF16), jax.ShapeDtypeStruct((8, 128), F32)],
        in_specs=[SMEM, ANY] + [VMEM] * (2 + len(sums)),
        out_specs=[VMEM, VMEM],
        compiler_params=pltpu.CompilerParams(vmem_limit_bytes=6 << 20),
        name="update",
    )(place, after, stream, stream_sib, *sums)


def stage_kernel(place_ref, own_ref, sib_ref, both_ref, mark_ref, sems):
    ranks = sems.shape[1]
    part, width = own_ref.shape[0] // ranks, own_ref.shape[1]
    mark_ref[...] = jnp.zeros(mark_ref.shape, F32)
    if width % 128:
        for k in range(ranks):
            source = pl.ds(pl.multiple_of((place_ref[0] ^ k) * part, part), part) if ranks > 1 else slice(0, part)
            both_ref[k * part : (k + 1) * part, :width] = own_ref[source, :]
            both_ref[k * part : (k + 1) * part, width:] = sib_ref[source, :]
        return
    copies = []
    for k in range(ranks):
        source = pl.ds(pl.multiple_of((place_ref[0] ^ k) * part, part), part) if ranks > 1 else slice(0, part)
        target = slice(k * part, (k + 1) * part)
        copies.append(pltpu.make_async_copy(own_ref.at[source], both_ref.at[target, :width], sems.at[0, k]))
        copies.append(pltpu.make_async_copy(sib_ref.at[source], both_ref.at[target, width:], sems.at[1, k]))
    for copy in copies:
        copy.start()
    for copy in copies:
        copy.wait()


def stage(place, own, sib, ranks):
    depth, width = own.shape
    return pl.pallas_call(
        stage_kernel,
        out_shape=[jax.ShapeDtypeStruct((depth, 2 * width), BF16), jax.ShapeDtypeStruct((8, 128), F32)],
        in_specs=[SMEM] + [VMEM if width % 128 else HBM] * 2,
        out_specs=[VMEM, VMEM],
        scratch_shapes=[pltpu.SemaphoreType.DMA((2, ranks))],
        compiler_params=pltpu.CompilerParams(vmem_limit_bytes=(8 if width % 128 else 4) * depth * width + (4 << 20)),
        name="stage",
    )(place, own, sib)


def score_kernel(chips, tp_count, own_rows, blocks, first, place_ref, after_ref, ready_ref, tokens_ref, gain_ref, head_ref, *refs):
    pieces, out_ref, normed = refs[:-2], refs[-2], refs[-1]
    if first:
        pieces, earlier_ref = pieces[:-1], pieces[-1]
    spans = len(pieces) // chips
    ctx, tp = place_ref[0], place_ref[1]
    ranks = 2 * chips
    part, vocab = head_ref.shape[0] // ranks, head_ref.shape[1] // 2
    span_rows = pieces[0].shape[0]
    squares = [jnp.zeros((span_rows, 1), F32)] * spans
    for j in range(chips):
        gain = jnp.concatenate([gain_ref[pl.ds(ctx ^ (2 * j), 1), :], gain_ref[pl.ds(ctx ^ (2 * j + 1), 1), :]], axis=1)
        for s in range(spans):
            wide = pieces[s * chips + j][...].astype(F32)
            squares[s] += jnp.sum(wide * wide, axis=1, keepdims=True)
            normed[s * span_rows : (s + 1) * span_rows, 2 * j * part : 2 * (j + 1) * part] = (wide * gain).astype(BF16)
    square = jnp.concatenate(squares, axis=0)
    inverse = lax.rsqrt(square * (1.0 / (ranks * part)) + EPSILON)
    logits = jnp.dot(normed[...], head_ref[...], preferred_element_type=F32) * inverse
    rows = logits.shape[0]
    column = lax.broadcasted_iota(jnp.int32, (1, 2 * vocab), 1)
    offset = jnp.where(column < vocab, (ctx * tp_count + tp) * vocab, ((ctx ^ 1) * tp_count + tp) * vocab - vocab)
    owners = [
        (tp ^ k) * blocks + 2 * b + lax.rem(ctx, 2) for k in range(first, first + spans) for b in range(blocks // 2)
    ]
    length = tokens_ref.shape[1]
    line = lax.broadcasted_iota(jnp.int32, (own_rows, length), 1) - lax.broadcasted_iota(jnp.int32, (own_rows, length), 0)
    tokens = jnp.concatenate(
        [
            jnp.sum(jnp.where(line == owner * own_rows, tokens_ref[...], 0), axis=1, keepdims=True)
            for owner in owners
        ],
        axis=0,
    )
    highest = jnp.max(logits, axis=1, keepdims=True)
    total = jnp.sum(jnp.exp(logits - highest), axis=1, keepdims=True)
    target = jnp.sum(jnp.where(column + offset == tokens, logits, 0.0), axis=1, keepdims=True)
    lane = lax.broadcasted_iota(jnp.int32, (rows, 128), 1)
    packed = jnp.where(lane == 0, highest, jnp.where(lane == 1, total, jnp.where(lane == 2, target, 0.0)))
    turned = packed.T[:4]
    out_ref[...] = earlier_ref[...] if first else jnp.zeros(out_ref.shape, F32)
    for i, owner in enumerate(owners):
        tile = turned[:, i * own_rows : (i + 1) * own_rows]
        for k in range(tp_count):
            out_ref[pl.ds(owner * tp_count + k, 1), :, :own_rows] = tile[None]


def score(place, after, ready, tokens, gain, head, spans, first, earlier, tp_count, own_rows, blocks):
    chips = len(spans[0])
    rows = len(spans) * spans[0][0].shape[0]
    depth, vocab = head.shape
    need = 2 * depth * vocab + rows * depth * 6 + rows * vocab * 4 * 8
    return pl.pallas_call(
        lambda *refs: score_kernel(chips, tp_count, own_rows, blocks, first, *refs),
        out_shape=jax.ShapeDtypeStruct((2 * chips * tp_count, 4, 128), F32),
        in_specs=[SMEM, ANY, ANY] + [VMEM] * (3 + len(spans) * chips + len(earlier)),
        out_specs=VMEM,
        scratch_shapes=[pltpu.VMEM((rows, depth), BF16)],
        compiler_params=pltpu.CompilerParams(vmem_limit_bytes=need + (12 << 20)),
        name="score",
    )(place, after, ready, tokens, gain, head, *[piece for span in spans for piece in span], *earlier)


def merge_kernel(chips, tp_count, place_ref, policy_ref, stats_ref, logprob_ref, penalty_ref):
    parity = lax.rem(place_ref[0], 2)
    own_rows = policy_ref.shape[1]
    tiles = [
        stats_ref[(2 * j + parity) * tp_count + k] for j in range(chips) for k in range(tp_count)
    ]
    highest = tiles[0][0:1]
    for tile in tiles[1:]:
        highest = jnp.maximum(highest, tile[0:1])
    total = jnp.zeros_like(highest)
    target = jnp.zeros_like(highest)
    for tile in tiles:
        total += tile[1:2] * jnp.exp(tile[0:1] - highest)
        target += tile[2:3]
    logprob = (target - (highest + jnp.log(total)))[:, :own_rows]
    ratio = logprob - policy_ref[...]
    logprob_ref[...] = logprob
    penalty_ref[...] = jnp.minimum(jnp.exp(ratio) - ratio - 1.0, CEILING)


def merge(place, policy, stats, chips, tp_count):
    shape = jax.ShapeDtypeStruct(policy.shape, F32)
    return pl.pallas_call(
        lambda *refs: merge_kernel(chips, tp_count, *refs),
        out_shape=[shape, shape],
        in_specs=[SMEM, VMEM, VMEM],
        out_specs=[VMEM, VMEM],
        compiler_params=pltpu.CompilerParams(vmem_limit_bytes=4 << 20),
        name="merge",
    )(place, policy, stats)


def local(
    queries,
    key_rows,
    value_rows,
    out_weight,
    stream,
    final_gain,
    head_weight,
    token_ids,
    policy_logprob,
    doc_lengths,
    slab_start,
):
    ctx_count, tp_count = lax.axis_size("ctx"), lax.axis_size("tp")
    ctx, tp = lax.axis_index("ctx"), lax.axis_index("tp")
    chips = ctx_count // 2
    own_rows = queries.shape[0]
    blocks = ctx_count // tp_count
    mid = tp_count // 2
    place = jnp.stack([ctx, tp, slab_start[0]]).astype(jnp.int32)

    together = jnp.concatenate([queries, key_rows, value_rows], axis=1)
    low, high = pack(together, swap(key_rows, "ctx", 1), swap(value_rows, "ctx", 1))
    low, high, out_weight, stream = lax.optimization_barrier((low, high, out_weight, stream))
    sets = list(zip(corners(sides(low, chips), 0), corners(sides(high, chips), 1)))
    out_sibling, stream_sibling = swap(out_weight, "ctx", 1), swap(stream, "ctx", 1)
    weight, mark = stage(place, out_weight, out_sibling, 1)
    mark, stream_sibling = lax.optimization_barrier((mark, stream_sibling))

    lens, kv_width = doc_lengths[None], key_rows.shape[1]
    far = attend(place, mark, lens, sets, kv_width, weight, range(mid, tp_count), tp_count, blocks)
    head_weight, *far = lax.optimization_barrier((head_weight, *far))
    head_sibling = swap(head_weight, "ctx", 1)
    near = attend(place, far[0], lens, sets, kv_width, weight, range(mid), tp_count, blocks)
    sums = [*near, *far]
    received = [swap(sums[k], "tp", k) for k in range(1, tp_count)]
    gain, tokens, sums[0] = lax.optimization_barrier((final_gain, token_ids, sums[0]))
    gain, tokens = gain.astype(F32).reshape(ctx_count, -1), tokens[None]
    sums[0], gain, tokens, head_sibling = lax.optimization_barrier((sums[0], gain, tokens, head_sibling))
    updated, mark = update(place, gain, stream, stream_sibling, [sums[0]] + received, blocks, own_rows)
    here, mark, head_sibling = lax.optimization_barrier((updated, swap(mark, "ctx", 1), head_sibling))
    head, ready = stage(place, head_weight, head_sibling, ctx_count)
    pieces, spans = [updated], []
    for k in range(1, tp_count):
        step = k & -k
        if step < k:
            pieces[k - step], ready = lax.optimization_barrier((pieces[k - step], ready))
        pieces.append(swap(pieces[k - step], "tp", step))
    for k, piece in enumerate([here] + pieces[1:]):
        if k == 1 and chips == 4:
            spans.append([piece] + [swap(one, "tp", 1) for one in spans[0][1:]])
        else:
            spans.append(sides(piece, chips))
    for k in range(tp_count):
        if k == 1 and chips == 4:
            spans[k].append(swap(spans[0][3], "tp", 1))
        else:
            spans[k] = corners(spans[k], k % 2)
    sizes = (tp_count, own_rows, blocks)
    stats = score(place, mark, ready, tokens, gain, head, spans[:mid], 0, [], *sizes)
    stats = score(place, mark, ready, tokens, gain, head, spans[mid:], mid, [stats], *sizes)
    stats = lax.all_to_all(stats, ("ctx", "tp"), 0, 0, tiled=True)
    logprob, penalty = merge(place, policy_logprob[None], stats, chips, tp_count)
    return (logprob[0], penalty[0])


def solution(mesh):
    placed = (
        P("ctx", "tp"),
        P("ctx", "tp"),
        P("ctx", "tp"),
        P("tp", "ctx"),
        P("tp", "ctx"),
        P(),
        P(None, ("ctx", "tp")),
        P(),
        P("ctx"),
        P(),
        P(),
    )
    return jax.shard_map(
        local, mesh=mesh, in_specs=placed, out_specs=(P("ctx"), P("ctx")), check_vma=False
    )
```
